256 devices in a mesh: tm: 32 (over x, z), dp: 8 (over y, core).
Axes of the slice: x: 4, y: 4, z: 8, core: 2. Of those that a mesh axis runs over, the one named last changes fastest.
Arguments:
- features: float32 [8, 32, 32, 128], P('dp'), may hold values from -6 to 6
- cotangent: float32 [8, 32, 32, 128], P('dp'), may hold values from -6 to 6
- weights: bfloat16 [64, 9, 128, 128], P('tm'), may hold values from -0.1875 to 0.1875
- coarse_map: float32 [32, 128, 128], P('tm'), may hold values from -0.05 to 0.05
Outputs:
- boundary_states: float32 [32, 8, 32, 32, 128], P('tm', 'dp')
- adjoint_states: float32 [32, 8, 32, 32, 128], P('tm', 'dp')
- weight_grad: float32 [64, 9, 128, 128], P('tm')
The draws below stay inside these ranges and needn't reach their ends.
All inputs are finite; a program needn't handle non-finite values.
Results may differ from the reference program's by a relative error of at most 0.0045.
Values sent between devices are 32-bit elements; how exact they have to be, the bound alone decides.
A program may use at most 128 MiB of HBM per device.

```python
import jax
import jax.numpy as jnp
from jax import lax

CH = 128
MAP = 32
CYCLES = 2
INTERVALS = 32
LAYERS = 64
BATCH = 8


def draw_coarse_map(key, part):
    key = jax.random.fold_in(key, 7)
    shape = (INTERVALS, CH, CH)
    values = jnp.clip(0.008 * jax.random.normal(key, shape, jnp.float32), -0.05, 0.05)
    return values


def levels(rng, shape, cuts, low, largest):
    level, own = 1.0, jax.random.fold_in(rng, 6)
    for axis_at, parts in cuts:
        steps = jnp.exp(jax.random.uniform(jax.random.fold_in(own, axis_at), (parts,), jnp.float32, low / len(cuts), largest / len(cuts)))
        level = level * jnp.repeat(steps, shape[axis_at] // parts).reshape([-1 if axis == axis_at else 1 for axis in range(len(shape))])
    return level


def scatter_about(rng, shape, scale, reach, shards=(), kind=jnp.bfloat16):
    drawn = jax.random.normal(rng, shape, jnp.float32) * scale
    if len(shards) > 0:
        drawn = levels(rng, shape, shards, -0.22, 0.18) * drawn
    return jnp.clip(drawn, min=-reach, max=reach).astype(kind)


def setup_inputs(seed: int = 0) -> dict:
    key_list = jax.random.split(jax.random.key(seed), 5)
    return {
        "features": scatter_about(key_list[0], (BATCH, MAP, MAP, CH), 1.0, 6.0, ((0, 8),), jnp.float32),
        "cotangent": scatter_about(key_list[1], (BATCH, MAP, MAP, CH), 1.0, 6.0, ((0, 8),), jnp.float32),
        "weights": scatter_about(key_list[2], (LAYERS, 9, CH, CH), (9 * CH) ** -0.5, 0.1875, ((0, 32),)),
        "coarse_map": draw_coarse_map(jax.random.fold_in(key_list[4], 71), 0),
    }


step_size = 0.25
coarse_diagonal = 0.9

def pad_map(values):
    return jnp.pad(values, ((0, 0), (1, 1), (1, 1), (0, 0)))

def tap_slices(padded, height, breadth, flipped):
    pieces = []
    for tap_index in range(9):
        tap_row = tap_index // 3
        tap_col = tap_index % 3
        if flipped:
            tap_row = 2 - tap_row
            tap_col = 2 - tap_col
        pieces.append(padded[:, tap_row:tap_row + height, tap_col:tap_col + breadth, :])
    return pieces

def convolve(active, kernel):
    images, height, breadth, channels = active.shape
    summed = jnp.zeros((images * height * breadth, kernel.shape[2]), jnp.float32)
    for tap_index, piece in enumerate(tap_slices(pad_map(active), height, breadth, False)):
        summed = summed + jnp.dot(piece.reshape(-1, channels), kernel[tap_index], preferred_element_type=jnp.float32)
    return summed.reshape(images, height, breadth, -1)

def convolve_back(signal, kernel):
    images, height, breadth, channels = signal.shape
    summed = jnp.zeros((images * height * breadth, kernel.shape[1]), jnp.float32)
    for tap_index, piece in enumerate(tap_slices(pad_map(signal), height, breadth, True)):
        summed = summed + jnp.dot(piece.reshape(-1, channels), kernel[tap_index].T, preferred_element_type=jnp.float32)
    return summed.reshape(images, height, breadth, -1)

def kernel_grad(active, signal):
    images, height, breadth, channels = active.shape
    flat_signal = signal.reshape(-1, signal.shape[3])
    blocks = []
    for piece in tap_slices(pad_map(active), height, breadth, False):
        blocks.append(lax.dot_general(piece.reshape(-1, channels), flat_signal, (((0,), (0,)), ((), ())), preferred_element_type=jnp.float32))
    return jnp.stack(blocks, 0)

def forward_step(current, kernel):
    return current + step_size * convolve(jnp.tanh(current).astype(jnp.bfloat16), kernel)

def adjoint_step(current, signal, kernel):
    active = jnp.tanh(current)
    return signal + step_size * (1.0 - active * active) * convolve_back(signal.astype(jnp.bfloat16), kernel)

def apply_map(vector, matrix):
    flat = jnp.dot(vector.reshape(-1, vector.shape[-1]), matrix, precision=lax.Precision.HIGHEST, preferred_element_type=jnp.float32)
    return flat.reshape(vector.shape)

def coarse_solve(residual, matrices, backward):

    def advance(carried, pair):
        updated = apply_map(carried, pair[0]) + pair[1]
        return (updated, updated)
    _, corrections = lax.scan(advance, jnp.zeros(residual.shape[1:], jnp.float32), (matrices, residual), reverse=backward)
    return corrections

def reference(features, cotangent, weights, coarse_map):
    intervals = coarse_map.shape[0]
    channels = coarse_map.shape[1]
    layers_dev = weights.shape[0] // intervals
    kernels = weights.reshape(intervals, layers_dev, 9, channels, channels)
    coarse_maps = coarse_diagonal * jnp.eye(channels, dtype=jnp.float32)[None] + coarse_map
    backward_maps = jnp.transpose(coarse_maps, (0, 2, 1))
    batched_step = jax.vmap(forward_step)
    batched_adjoint = jax.vmap(adjoint_step)
    batched_grad = jax.vmap(kernel_grad)

    def relax_forward(ends):
        current = jnp.concatenate([features[None], ends[:-1]], 0)
        states = []
        for layer_index in range(layers_dev):
            states.append(current)
            current = batched_step(current, kernels[:, layer_index])
        return (current, states)
    ends = jnp.broadcast_to(features, (intervals,) + features.shape)
    for cycle_index in range(CYCLES):
        propagated, _ = relax_forward(ends)
        ends = ends + coarse_solve(propagated - ends, coarse_maps, False)
    _, states = relax_forward(ends)

    def adjoint_ends(adjoint):
        return jnp.concatenate([adjoint[1:], cotangent[None]], 0)
    adjoint = jnp.broadcast_to(cotangent, (intervals,) + cotangent.shape)
    for cycle_index in range(CYCLES):
        current = adjoint_ends(adjoint)
        for layer_index in reversed(range(layers_dev)):
            current = batched_adjoint(states[layer_index], current, kernels[:, layer_index])
        adjoint = adjoint + coarse_solve(current - adjoint, backward_maps, True)
    current = adjoint_ends(adjoint)
    gradients = [None] * layers_dev
    for layer_index in reversed(range(layers_dev)):
        gradients[layer_index] = batched_grad(jnp.tanh(states[layer_index]).astype(jnp.bfloat16), current.astype(jnp.bfloat16))
        if layer_index > 0:
            current = batched_adjoint(states[layer_index], current, kernels[:, layer_index])
    weight_grad = jnp.stack(gradients, 1).reshape(weights.shape) * (step_size / BATCH)
    return (ends, adjoint, weight_grad)
```

```python
import functools

import jax
import jax.numpy as jnp
from jax import lax
from jax.experimental import pallas as pl
from jax.experimental.pallas import tpu as pltpu
from jax.sharding import PartitionSpec as P

MESH = pl.DeviceIdType.MESH
STEP = 0.25
DIAGONAL = 0.9
SIDE = 32
PIXELS = SIDE * SIDE
CH = 128
BANDS = 2
EDGES = ((0, 22, 32), (0, 20, 32), (0, 18, 32), (0, 16, 32))
TAPS = 9 * CH
F32, BF16 = jnp.float32, jnp.bfloat16


def two_terms(value):
    high = value.astype(BF16)
    return high, (value - high.astype(F32)).astype(BF16)


def times(value, tile):
    high, low = two_terms(value)
    both = jnp.dot(jnp.concatenate([high, low], 1), tile, preferred_element_type=F32)
    return both[:, :CH] + both[:, CH:]


def split(first, last, most=10):
    count = -(-(last - first) // most)
    cuts = [first + (last - first) * n // count for n in range(count + 1)]
    return list(zip(cuts[:-1], cuts[1:]))


def body(
    NX, NZ, NY, NC, factor,
    feat_in, cot_in, w_in, cm_in,
    ends, adj, grad,
    feat, cot, w, cm,
    x3a, x3b, z3a, z3b, wt, start, mid, prop, d0, d1, ycot, zt, zt0,
    resout, resin, eout, ein, tin, gin, pin, prods, temps, maps, segs, local_grad, gs, hsum, yin,
    in_s,
    res_s, res_r, e_s, e_r, t_s, t_r, g_s, g_r, gf_s, gf_r, p_s, p_r, sib_s, sib_r, rs_s, rs_r, ag_s, ag_r, fw_s, fw_r,
):
    loads = [
        pltpu.make_async_copy(src, dst, in_s.at[n])
        for n, (src, dst) in enumerate(((cm_in, cm), (feat_in, feat), (w_in, w), (cot_in, cot)))
    ]
    for load in loads:
        load.start()

    tm, dp = lax.axis_index("tm"), lax.axis_index("dp")
    x, z = tm // NZ, lax.rem(tm, NZ)
    y, c = dp // NC, lax.rem(dp, NC)
    half = TAPS // NC
    part = half // NY
    far_first = sorted(range(1, NZ), key=lambda d: -min(d, NZ - d))

    def to_z(d):
        return {"tm": x * NZ + lax.rem(z + d, NZ)}

    def to_x(d):
        return {"tm": lax.rem(x + d, NX) * NZ + z}

    def to_y(d):
        return {"dp": lax.rem(y + d, NY) * NC + c}

    def to_core():
        return {"dp": y * NC + (NC - 1 - c)}

    def remote(src, dst, send, recv, device):
        return pltpu.make_async_remote_copy(
            src_ref=src, dst_ref=dst, send_sem=send, recv_sem=recv, device_id=device, device_id_type=MESH
        )

    def each(count, f, first=0):
        def go(i, carry):
            f(i)
            return carry
        lax.fori_loop(first, count, go, 0)

    barrier = pltpu.get_barrier_semaphore()

    def greet(device):
        pl.semaphore_signal(barrier, inc=1, device_id=device, device_id_type=MESH)

    each(NZ, lambda d: greet(to_z(d)), 1)
    each(NX, lambda d: greet(to_x(d)), 1)
    each(NY, lambda d: greet(to_y(d)), 1)
    greet(to_core())

    def px(first, last):
        return slice(first * SIDE, last * SIDE)

    def fill(buffer, first, last, value):
        size = (last - first) * SIDE
        column = lax.rem(lax.broadcasted_iota(jnp.int32, (size, CH), 0), SIDE)
        left = jnp.where(column == 0, 0.0, pltpu.roll(value, 1, 0))
        right = jnp.where(column == SIDE - 1, 0.0, pltpu.roll(value, size - 1, 0))
        at = px(first + 1, last + 1)
        buffer[at, :CH] = left.astype(BF16)
        buffer[at, CH : 2 * CH] = value.astype(BF16)
        buffer[at, 2 * CH :] = right.astype(BF16)

    def conv(buffer, first, last, kernel):
        pieces = [buffer[px(first + r, last + r), :] for r in range(3)]
        return jnp.dot(jnp.concatenate(pieces, 1), kernel, preferred_element_type=F32)

    zero_row = jnp.zeros((SIDE, 3 * CH), BF16)
    for buffer in (x3a, x3b, z3a, z3b):
        buffer[:SIDE, :] = zero_row
        buffer[PIXELS + SIDE :, :] = zero_row
    eye = (lax.broadcasted_iota(jnp.int32, (CH, CH), 0) == lax.broadcasted_iota(jnp.int32, (CH, CH), 1)).astype(F32)
    loads[0].wait()
    gin[z] = DIAGONAL * eye + cm[...]

    loads[1].wait()
    for p, q in split(0, SIDE):
        value = feat[px(p, q), :]
        start[px(p, q), :] = value
        fill(x3a, p, q, jnp.tanh(value))
    loads[2].wait()
    pl.semaphore_wait(barrier, NZ - 1 + NX - 1 + NY - 1 + 1)

    gh = pl.ds(pl.multiple_of(c * (CH // NC), CH // NC), CH // NC)

    def g_copy(d):
        return remote(gin.at[z, gh], gin.at[z, gh], g_s.at[d], g_r.at[d], to_z(d))

    def g_forward(d):
        zs = lax.rem(z + NZ - d, NZ)
        return remote(gin.at[zs, gh], gin.at[zs, gh], gf_s.at[d], gf_r.at[d], to_core())

    for d in far_first:
        g_copy(d).start()

    def share(k, b):
        first, last = EDGES[k][b], EDGES[k][b + 1]
        return first * SIDE, (last - first) * SIDE // NZ

    def spot(k, b, n):
        base, R = share(k, b)
        if isinstance(n, int):
            return slice(base + n * R, base + n * R + R)
        return pl.ds(pl.multiple_of(base + n * R, 8), R)

    def res_copy(k, b, d):
        zp = lax.rem(z + d, NZ)
        m = BANDS * k + b
        return remote(
            resout.at[k, spot(k, b, zp)], resin.at[k, spot(k, b, z)], res_s.at[m, d], res_r.at[m, d], to_z(d)
        )

    def send_residual(k, b):
        for d in far_first:
            res_copy(k, b, d).start()
        resin[k, spot(k, b, z), :] = resout[k, spot(k, b, z), :]

    def t_spot(k, b):
        base, R = share(k, b)
        return slice(base // NZ, base // NZ + R)

    def t_copy(k, b, d):
        m = BANDS * k + b
        at = t_spot(k, b)
        return remote(tin.at[k, x, at], tin.at[k, x, at], t_s.at[m, d], t_r.at[m, d], to_x(d))

    def e_copy(k, b, d):
        zp = lax.rem(z + d, NZ)
        m = BANDS * k + b
        return remote(eout.at[k, spot(k, b, zp)], ein.at[k, spot(k, b, z)], e_s.at[m, d], e_r.at[m, d], to_z(d))

    def put(where, index, matrix):
        high, low = two_terms(matrix)
        where[(*index, slice(0, CH), slice(0, CH))] = high
        where[(*index, slice(0, CH), slice(CH, None))] = low
        where[(*index, slice(CH, None), slice(0, CH))] = high
        where[(*index, slice(CH, None), slice(CH, None))] = jnp.zeros((CH, CH), BF16)

    def scan(k, b, backward):
        total_kind, chain_kind, carry_kind = (3, 1, 5) if backward else (4, 0, 2)
        at = t_spot(k, b)
        edge = NZ - 1 if backward else 0
        for d in far_first[::-1]:
            res_copy(k, b, d).wait_recv()
        inner = NZ - 1 - edge
        total = resin[k, spot(k, b, inner), :]
        for s in range(NZ):
            if s != inner:
                total = total + times(resin[k, spot(k, b, s), :], maps[total_kind, s + (0 if backward else 1)])
        tin[k, x, at, :] = total
        for d in range(1, NX):
            t_copy(k, b, d).start()
        run = {}
        if backward:
            value = resin[k, spot(k, b, NZ - 1), :]
            run[NZ - 2] = value
            for s in range(NZ - 2, 0, -1):
                value = times(value, maps[chain_kind, s]) + resin[k, spot(k, b, s), :]
                run[s - 1] = value
        else:
            value = resin[k, spot(k, b, 0), :]
            run[1] = value
            for s in range(1, NZ - 1):
                value = times(value, maps[chain_kind, s]) + resin[k, spot(k, b, s), :]
                run[s + 1] = value
        for n in run:
            eout[k, spot(k, b, n), :] = run[n]
        if (k, b) == (0, 0):
            segments_arrive()
        for d in range(1, NX):
            t_copy(k, b, d).wait_recv()
        if backward:
            carry = jnp.where(x < NX - 1, tin[k, NX - 1, at, :], 0.0)
            for xs in range(NX - 2, 0, -1):
                carry = jnp.where(x < xs, times(carry, segs[1, xs]) + tin[k, xs, at, :], carry)
        else:
            carry = jnp.where(x > 0, tin[k, 0, at, :], 0.0)
            for xs in range(1, NX - 1):
                carry = jnp.where(x > xs, times(carry, segs[0, xs]) + tin[k, xs, at, :], carry)
        for n in range(NZ):
            if n == edge:
                eout[k, spot(k, b, n), :] = carry
            else:
                tile = maps[carry_kind, n + (1 if backward else 0)]
                eout[k, spot(k, b, n), :] = eout[k, spot(k, b, n), :] + times(carry, tile)
        for d in far_first:
            e_copy(k, b, d).start()
        ein[k, spot(k, b, z), :] = eout[k, spot(k, b, z), :]

    def arrive(k, b):
        for d in far_first[::-1]:
            e_copy(k, b, d).wait_recv()

    def relax(k, b, ahead, old):
        first, last = EDGES[k][b], EDGES[k][b + 1]
        lo = 0 if b == 0 else first + ahead
        hi = SIDE if b == BANDS - 1 else last + ahead
        for p, q in split(lo, hi):
            value = start[px(p, q), :] + STEP * conv(x3a, p, q, w[0])
            mid[px(p, q), :] = value
            fill(x3b, p, q, jnp.tanh(value))
        for p, q in split(first, last):
            value = mid[px(p, q), :] + STEP * conv(x3b, p, q, w[1])
            prop[px(p, q), :] = value
            resout[k, px(p, q), :] = value - old[px(p, q), :]
        send_residual(k, b)


    relax(0, 0, 1, feat)

    def g_pass(d):
        g_copy(d).wait_recv()
        g_forward(d).start()

    each(NZ, g_pass, 1)
    for b in range(1, BANDS):
        relax(0, b, 1, feat)

    each(NZ, lambda d: g_forward(d).wait_recv(), 1)
    made, tiles = {}, {}

    def product(i, j):
        if (i, j) not in made:
            if i == j:
                value = gin[i]
            else:
                step = 1
                while (j // (2 * step)) * 2 * step > i:
                    step *= 2
                m = j // step * step
                value = times(product(i, m - 1), tile_of(m, j))
            made[i, j] = value
        return made[i, j]

    def tile_of(i, j):
        if (i, j) not in tiles:
            value = product(i, j)
            if i == j:
                put(maps, (0, i), value)
                tiles[i, j] = maps.at[0, i]
            elif j == NZ - 1:
                put(maps, (4, i), value)
                tiles[i, j] = maps.at[4, i]
            else:
                n = sum(i2 != j2 and j2 != NZ - 1 for i2, j2 in tiles)
                put(temps, (n,), value)
                tiles[i, j] = temps.at[n]
        return tiles[i, j][...]

    for n in range(NZ):
        tile_of(n, n)
    put(maps, (4, NZ), eye)
    put(maps, (4, NZ - 1), gin[NZ - 1])
    for n in range(NZ - 1):
        tile_of(n, NZ - 1)
    for n in range(NZ):
        prods[1, n] = product(n, NZ - 1)
        prods[0, n + 1] = product(0, n)
        put(maps, (2, n + 1), product(0, n))
    pin[x] = product(0, NZ - 1)

    def p_copy(d):
        return remote(pin.at[x], pin.at[x], p_s.at[d], p_r.at[d], to_x(d))

    each(NX, lambda d: p_copy(d).start(), 1)

    def segments_arrive():
        each(NX, lambda d: p_copy(d).wait_recv(), 1)
        for xs in range(1, NX - 1):
            put(segs, (0, xs), pin[xs])

    for b in range(BANDS):
        scan(0, b, False)

    def turn_kernels(layer):
        def turn(t):
            block = w[layer, pl.ds(pl.multiple_of((8 - t) * CH, CH), CH), :].astype(F32)
            wt[layer, pl.ds(pl.multiple_of(t * CH, CH), CH), :] = block.T.astype(BF16)
        each(9, turn)

    turn_kernels(1)
    turn_kernels(0)

    for b in range(BANDS):
        arrive(0, b)
        for p, q in split(EDGES[0][b], EDGES[0][b + 1]):
            e = ein[0, px(p, q), :]
            ends[px(p, q), :] = prop[px(p, q), :] + times(e, maps[0, z])
            value = start[px(p, q), :] + e
            start[px(p, q), :] = value
            fill(x3a, p, q, jnp.tanh(value))
        relax(1, b, 1, ends)

    loads[3].wait()
    for p, q in split(0, SIDE):
        fill(z3a, p, q, cot[px(p, q), :])
    for p, q in split(0, SIDE):
        ycot[px(p, q), :] = conv(z3a, p, q, wt[1])

    for b in range(BANDS):
        scan(1, b, False)

    def turn_maps(s):
        put(maps, (3, s + 1), prods[0, s + 1].T)

    put(maps, (3, 0), eye)
    each(NZ - 1, turn_maps)

    def pull(k, b, old):
        first, last = EDGES[k][b], EDGES[k][b + 1]
        for p, q in split(first, last):
            value = mid[px(p, q), :] + d0[px(p, q), :] * conv(z3b, p, q, wt[0])
            prop[px(p, q), :] = value
            resout[k, px(p, q), :] = value - old[px(p, q), :]
        send_residual(k, b)

    def behind(k, b):
        lo = 0 if b == 0 else EDGES[k][b] + 1
        hi = SIDE if b == BANDS - 1 else EDGES[k][b + 1] + 1
        return split(lo, hi)

    for b in range(BANDS):
        arrive(1, b)
        for p, q in split(EDGES[1][b], EDGES[1][b + 1]):
            e = ein[1, px(p, q), :]
            ends[px(p, q), :] = prop[px(p, q), :] + times(e, maps[0, z])
            value = start[px(p, q), :] + e
            start[px(p, q), :] = value
            active = jnp.tanh(value)
            d0[px(p, q), :] = STEP * (1.0 - active * active)
            fill(x3a, p, q, active)
        for p, q in behind(2, b):
            active = jnp.tanh(start[px(p, q), :] + STEP * conv(x3a, p, q, w[0]))
            slope = STEP * (1.0 - active * active)
            d1[px(p, q), :] = slope
            fill(x3b, p, q, active)
            value = cot[px(p, q), :] + slope * ycot[px(p, q), :]
            mid[px(p, q), :] = value
            fill(z3b, p, q, value)
        pull(2, b, cot)

    def turn_more_maps(s):
        put(maps, (1, s), gin[s].T)
        put(maps, (5, s), prods[1, s].T)

    each(NZ, turn_more_maps)
    for xs in range(1, NX - 1):
        put(segs, (1, xs), pin[xs].T)

    for b in range(BANDS):
        scan(2, b, True)

    for b in range(BANDS):
        arrive(2, b)
        for p, q in split(EDGES[2][b], EDGES[2][b + 1]):
            f = ein[2, px(p, q), :]
            adj[px(p, q), :] = prop[px(p, q), :] + times(f, maps[1, z])
            value = cot[px(p, q), :] + f
            start[px(p, q), :] = value
            fill(z3a, p, q, value)
        for p, q in behind(3, b):
            value = start[px(p, q), :] + d1[px(p, q), :] * conv(z3a, p, q, wt[1])
            mid[px(p, q), :] = value
            fill(z3b, p, q, value)
        pull(3, b, adj)

    for b in range(BANDS):
        scan(3, b, True)

    def place(core, yy):
        return pl.ds(pl.multiple_of(core * half + yy * part, part), part)

    other = pl.ds(pl.multiple_of((NC - 1 - c) * half, half), half)

    def sib_copy(layer):
        return remote(local_grad.at[layer, other], gs.at[layer], sib_s.at[layer], sib_r.at[layer], to_core())

    def rs_copy(layer, d):
        return remote(hsum.at[layer, lax.rem(y + d, NY)], yin.at[layer, d], rs_s.at[layer, d], rs_r.at[layer, d], to_y(d))

    def ag_copy(layer, d):
        at = place(c, y)
        return remote(grad.at[layer, at], grad.at[layer, at], ag_s.at[layer, d], ag_r.at[layer, d], to_y(d))

    def fw_copy(layer, d):
        at = place(c, lax.rem(y + NY - d, NY))
        return remote(grad.at[layer, at], grad.at[layer, at], fw_s.at[layer, d], fw_r.at[layer, d], to_core())

    def reduce_core(layer):
        sib_copy(layer).wait()
        for yy in range(NY):
            hsum[layer, yy] = local_grad[layer, place(c, yy), :] + gs[layer, pl.ds(yy * part, part), :]
        each(NY, lambda d: rs_copy(layer, d).start(), 1)

    def reduce_chips(layer):
        total = hsum[layer, y]
        for d in range(1, NY):
            rs_copy(layer, d).wait_recv()
            total = total + yin[layer, d]
        grad[layer, place(c, y), :] = total * factor
        each(NY, lambda d: ag_copy(layer, d).start(), 1)
        fw_copy(layer, 0).start()

    def spread(layer):
        def go(d):
            ag_copy(layer, d).wait_recv()
            fw_copy(layer, d).start()
        each(NY, go, 1)

    def gradient(layer, signal, buffer, first, last, more):
        for r in range(3):
            block = jnp.dot(signal[:, px(first, last)], buffer[px(first + r, last + r), :], preferred_element_type=F32)
            for s in range(3):
                t = 3 * r + s
                value = block[:, CH * s : CH * (s + 1)].T
                at = slice(CH * t, CH * (t + 1))
                local_grad[layer, at, :] = local_grad[layer, at, :] + value if more else value

    def adjoint_out(b):
        for p, q in split(EDGES[3][b], EDGES[3][b + 1]):
            adj[px(p, q), :] = prop[px(p, q), :] + times(ein[3, px(p, q), :], maps[1, z])

    def top_signal(p, q):
        value = start[px(p, q), :] + ein[3, px(p, q), :]
        start[px(p, q), :] = value
        fill(z3a, p, q, value)
        zt[:, px(p, q)] = value.T.astype(BF16)

    def lower_signal(p, q):
        value = start[px(p, q), :] + d1[px(p, q), :] * conv(z3a, p, q, wt[1])
        zt0[:, px(p, q)] = value.T.astype(BF16)

    cut = EDGES[3][1] // 4 * 4
    low = (EDGES[3][1] - 1) // 4 * 4
    arrive(3, 0)
    for p, q in split(0, cut, 8):
        top_signal(p, q)
    gradient(1, zt, x3b, 0, cut, False)
    for p, q in ((0, low // 8 * 4), (low // 8 * 4, low)):
        lower_signal(p, q)
    gradient(0, zt0, x3a, 0, low, False)
    adjoint_out(0)
    arrive(3, 1)
    for p, q in split(cut, SIDE, 8):
        top_signal(p, q)
    gradient(1, zt, x3b, cut, SIDE, True)
    sib_copy(1).start()
    for p, q in ((low, (low + SIDE) // 8 * 4), ((low + SIDE) // 8 * 4, SIDE)):
        lower_signal(p, q)
    gradient(0, zt0, x3a, low, SIDE, True)
    sib_copy(0).start()
    reduce_core(1)
    reduce_core(0)
    adjoint_out(1)
    reduce_chips(1)
    spread(1)
    reduce_chips(0)
    spread(0)
    for layer in range(2):
        each(NY, lambda d: fw_copy(layer, d).wait_recv(), 0)

    for layer in range(2):
        each(NY, lambda d: rs_copy(layer, d).wait_send(), 1)
        each(NY, lambda d: ag_copy(layer, d).wait_send(), 1)
        each(NY, lambda d: fw_copy(layer, d).wait_send(), 0)
    each(NZ, lambda d: g_copy(d).wait_send(), 1)
    each(NZ, lambda d: g_forward(d).wait_send(), 1)
    each(NX, lambda d: p_copy(d).wait_send(), 1)
    for k in range(4):
        for b in range(BANDS):
            each(NZ, lambda d: res_copy(k, b, d).wait_send(), 1)
            each(NZ, lambda d: e_copy(k, b, d).wait_send(), 1)
            each(NX, lambda d: t_copy(k, b, d).wait_send(), 1)


def make_local(NX, NZ, NY, NC):
    half = TAPS // NC
    part = half // NY
    dma = pltpu.SemaphoreType.DMA
    vmem = pltpu.VMEM
    image = vmem((PIXELS, CH), F32)
    padded = vmem((PIXELS + 2 * SIDE, 3 * CH), BF16)
    sweeps = vmem((4, PIXELS, CH), F32)
    moves = dma((4 * BANDS, NZ))

    def local(features, cotangent, weights, coarse_map):
        factor = STEP / (features.shape[0] * NY * NC)
        out = pl.pallas_call(
            functools.partial(body, NX, NZ, NY, NC, factor),
            out_shape=(
                jax.ShapeDtypeStruct((PIXELS, CH), F32),
                jax.ShapeDtypeStruct((PIXELS, CH), F32),
                jax.ShapeDtypeStruct((2, TAPS, CH), F32),
            ),
            in_specs=[pl.BlockSpec(memory_space=pl.ANY)] * 4,
            out_specs=[pl.BlockSpec(memory_space=vmem)] * 3,
            scratch_shapes=[
                image, image, vmem((2, TAPS, CH), BF16), vmem((CH, CH), F32),
                padded, padded, padded, padded,
                vmem((2, TAPS, CH), BF16),
                image, image, image, image, image, image,
                vmem((CH, PIXELS), BF16), vmem((CH, PIXELS), BF16),
                sweeps, sweeps, sweeps, sweeps,
                vmem((4, NX, PIXELS // NZ, CH), F32),
                vmem((NZ, CH, CH), F32),
                vmem((NX, CH, CH), F32),
                vmem((2, NZ + 1, CH, CH), F32),
                vmem((NZ, 2 * CH, 2 * CH), BF16),
                vmem((6, NZ + 1, 2 * CH, 2 * CH), BF16),
                vmem((2, NX, 2 * CH, 2 * CH), BF16),
                vmem((2, TAPS, CH), F32),
                vmem((2, half, CH), F32),
                vmem((2, NY, part, CH), F32),
                vmem((2, NY, part, CH), F32),
                dma((4,)),
                moves, moves, moves, moves, dma((4 * BANDS, NX)), dma((4 * BANDS, NX)),
                dma((NZ,)), dma((NZ,)), dma((NZ,)), dma((NZ,)), dma((NX,)), dma((NX,)),
                dma((2,)), dma((2,)), dma((2, NY)), dma((2, NY)), dma((2, NY)), dma((2, NY)), dma((2, NY)), dma((2, NY)),
            ],
            compiler_params=pltpu.CompilerParams(
                collective_id=0, has_side_effects=True, vmem_limit_bytes=56 * 1024 * 1024
            ),
            cost_estimate=pl.CostEstimate(flops=5 * 10**9, bytes_accessed=5 * 10**6, transcendentals=10**6),
        )(
            features.reshape(PIXELS, CH),
            cotangent.reshape(PIXELS, CH),
            weights.reshape(2, TAPS, CH),
            coarse_map.reshape(CH, CH),
        )
        shape = (1, 1, SIDE, SIDE, CH)
        return out[0].reshape(shape), out[1].reshape(shape), out[2].reshape(2, 9, CH, CH)

    return local


def build(mesh, sizes):
    return jax.shard_map(
        make_local(*sizes),
        mesh=mesh,
        in_specs=(P("dp", None, None, None), P("dp", None, None, None), P("tm", None, None, None), P("tm", None, None)),
        out_specs=(P("tm", "dp", None, None, None), P("tm", "dp", None, None, None), P("tm", None, None, None)),
        check_vma=False,
    )


def solution(mesh):
    return build(mesh, (4, 8, 4, 2))
```

```python
import functools

import jax
import jax.numpy as jnp
from jax import lax
from jax.experimental import pallas as pl
from jax.experimental.pallas import tpu as pltpu
from jax.sharding import PartitionSpec as P

MESH = pl.DeviceIdType.MESH
STEP = 0.25
DIAGONAL = 0.9
SIDE = 32
PIXELS = SIDE * SIDE
CH = 128
BANDS = 2
EDGES = ((0, 22, 32), (0, 20, 32), (0, 18, 32), (0, 16, 32))
TAPS = 9 * CH
F32, BF16 = jnp.float32, jnp.bfloat16


def two_terms(value):
    high = value.astype(BF16)
    return high, (value - high.astype(F32)).astype(BF16)


def times(value, tile):
    high, low = two_terms(value)
    both = jnp.dot(jnp.concatenate([high, low], 1), tile, preferred_element_type=F32)
    return both[:, :CH] + both[:, CH:]


def split(first, last, most=10):
    count = -(-(last - first) // most)
    cuts = [first + (last - first) * n // count for n in range(count + 1)]
    return list(zip(cuts[:-1], cuts[1:]))


def body(
    NX, NZ, NY, NC, factor,
    feat_in, cot_in, w_in, cm_in,
    ends, adj, grad,
    feat, cot, w, cm,
    x3a, x3b, z3a, z3b, wt, start, mid, prop, d0, d1, ycot, zt, zt0,
    resout, resin, eout, ein, tin, gin, pin, prods, temps, maps, segs, local_grad, gs, hsum, yin,
    in_s,
    relay, hop_s, hop_r, land_s, land_r,
    res_s, res_r, e_s, e_r, t_s, t_r, g_s, g_r, gf_s, gf_r, p_s, p_r, sib_s, sib_r, rs_s, rs_r, ag_s, ag_r, fw_s, fw_r,
):
    loads = [
        pltpu.make_async_copy(src, dst, in_s.at[n])
        for n, (src, dst) in enumerate(((cm_in, cm), (feat_in, feat), (w_in, w), (cot_in, cot)))
    ]
    for load in loads:
        load.start()

    tm, dp = lax.axis_index("tm"), lax.axis_index("dp")
    x, z = tm // NZ, lax.rem(tm, NZ)
    y, c = dp // NC, lax.rem(dp, NC)
    half = TAPS // NC
    part = half // NY
    opposite = NZ // 2 if NZ > 2 else 0
    far_first = sorted((d for d in range(1, NZ) if d != opposite), key=lambda d: -min(d, NZ - d))

    def to_z(d):
        return {"tm": x * NZ + lax.rem(z + d, NZ)}

    def to_x(d):
        return {"tm": lax.rem(x + d, NX) * NZ + z}

    def to_y(d):
        return {"dp": lax.rem(y + d, NY) * NC + c}

    def to_core():
        return {"dp": y * NC + (NC - 1 - c)}

    def remote(src, dst, send, recv, device):
        return pltpu.make_async_remote_copy(
            src_ref=src, dst_ref=dst, send_sem=send, recv_sem=recv, device_id=device, device_id_type=MESH
        )

    def each(count, f, first=0):
        def go(i, carry):
            f(i)
            return carry
        lax.fori_loop(first, count, go, 0)

    barrier = pltpu.get_barrier_semaphore()

    def greet(device):
        pl.semaphore_signal(barrier, inc=1, device_id=device, device_id_type=MESH)

    each(NZ, lambda d: greet(to_z(d)), 1)
    each(NX, lambda d: greet(to_x(d)), 1)
    each(NY, lambda d: greet(to_y(d)), 1)
    greet(to_core())

    def px(first, last):
        return slice(first * SIDE, last * SIDE)

    def fill(buffer, first, last, value):
        size = (last - first) * SIDE
        column = lax.rem(lax.broadcasted_iota(jnp.int32, (size, CH), 0), SIDE)
        left = jnp.where(column == 0, 0.0, pltpu.roll(value, 1, 0))
        right = jnp.where(column == SIDE - 1, 0.0, pltpu.roll(value, size - 1, 0))
        at = px(first + 1, last + 1)
        buffer[at, :CH] = left.astype(BF16)
        buffer[at, CH : 2 * CH] = value.astype(BF16)
        buffer[at, 2 * CH :] = right.astype(BF16)

    def conv(buffer, first, last, kernel):
        pieces = [buffer[px(first + r, last + r), :] for r in range(3)]
        return jnp.dot(jnp.concatenate(pieces, 1), kernel, preferred_element_type=F32)

    zero_row = jnp.zeros((SIDE, 3 * CH), BF16)
    for buffer in (x3a, x3b, z3a, z3b):
        buffer[:SIDE, :] = zero_row
        buffer[PIXELS + SIDE :, :] = zero_row
    eye = (lax.broadcasted_iota(jnp.int32, (CH, CH), 0) == lax.broadcasted_iota(jnp.int32, (CH, CH), 1)).astype(F32)
    loads[0].wait()
    gin[z] = DIAGONAL * eye + cm[...]

    loads[1].wait()
    for p, q in split(0, SIDE):
        value = feat[px(p, q), :]
        start[px(p, q), :] = value
        fill(x3a, p, q, jnp.tanh(value))
    loads[2].wait()
    pl.semaphore_wait(barrier, NZ - 1 + NX - 1 + NY - 1 + 1)

    gh = pl.ds(pl.multiple_of(c * (CH // NC), CH // NC), CH // NC)

    def g_copy(d):
        return remote(gin.at[z, gh], gin.at[z, gh], g_s.at[d], g_r.at[d], to_z(d))

    def g_forward(d):
        zs = lax.rem(z + NZ - d, NZ)
        return remote(gin.at[zs, gh], gin.at[zs, gh], gf_s.at[d], gf_r.at[d], to_core())

    for d in sorted(range(1, NZ), key=lambda d: -min(d, NZ - d)):
        g_copy(d).start()

    def share(k, b):
        first, last = EDGES[k][b], EDGES[k][b + 1]
        return first * SIDE, (last - first) * SIDE // NZ

    def spot(k, b, n):
        base, R = share(k, b)
        if isinstance(n, int):
            return slice(base + n * R, base + n * R + R)
        return pl.ds(pl.multiple_of(base + n * R, 8), R)

    def res_copy(k, b, d):
        zp = lax.rem(z + d, NZ)
        m = BANDS * k + b
        return remote(
            resout.at[k, spot(k, b, zp)], resin.at[k, spot(k, b, z)], res_s.at[m, d], res_r.at[m, d], to_z(d)
        )

    def send_residual(k, b):
        hop(0, k, b)
        for d in far_first:
            res_copy(k, b, d).start()
        resin[k, spot(k, b, z), :] = resout[k, spot(k, b, z), :]

    def t_spot(k, b):
        base, R = share(k, b)
        return slice(base // NZ, base // NZ + R)

    def t_copy(k, b, d):
        m = BANDS * k + b
        at = t_spot(k, b)
        return remote(tin.at[k, x, at], tin.at[k, x, at], t_s.at[m, d], t_r.at[m, d], to_x(d))

    def e_copy(k, b, d):
        zp = lax.rem(z + d, NZ)
        m = BANDS * k + b
        return remote(eout.at[k, spot(k, b, zp)], ein.at[k, spot(k, b, z)], e_s.at[m, d], e_r.at[m, d], to_z(d))

    def piece(k, b, n, side):
        base, R = share(k, b)
        cut = R // 16 * 8
        size = R - cut if side else cut
        return pl.ds(pl.multiple_of(base + n * R + (cut if side else 0), 8), size), size

    def ends_of(way):
        return (resout, resin) if way == 0 else (eout, ein)

    def hop_copy(way, k, b, side):
        m = BANDS * k + b
        at, size = piece(k, b, lax.rem(z + opposite, NZ), side)
        return remote(
            ends_of(way)[0].at[k, at], relay.at[way, m, side, :size],
            hop_s.at[way, m, side], hop_r.at[way, m, side], to_z(NZ - 1 if side else 1),
        )

    def land_copy(way, k, b, side):
        m = BANDS * k + b
        at, size = piece(k, b, lax.rem(z + (1 if side else NZ - 1), NZ), side)
        return remote(
            relay.at[way, m, side, :size], ends_of(way)[1].at[k, at],
            land_s.at[way, m, side], land_r.at[way, m, side], to_z(NZ - opposite + 1 if side else opposite - 1),
        )

    def hop(way, k, b):
        if opposite:
            for side in range(2):
                hop_copy(way, k, b, side).start()

    def pass_on(way, k, b):
        if opposite:
            for side in range(2):
                hop_copy(way, k, b, side).wait_recv()
                land_copy(way, k, b, side).start()

    def landed(way, k, b):
        if opposite:
            for side in range(2):
                land_copy(way, k, b, side).wait_recv()

    def put(where, index, matrix):
        high, low = two_terms(matrix)
        where[(*index, slice(0, CH), slice(0, CH))] = high
        where[(*index, slice(0, CH), slice(CH, None))] = low
        where[(*index, slice(CH, None), slice(0, CH))] = high
        where[(*index, slice(CH, None), slice(CH, None))] = jnp.zeros((CH, CH), BF16)

    def scan(k, b, backward):
        total_kind, chain_kind, carry_kind = (3, 1, 5) if backward else (4, 0, 2)
        at = t_spot(k, b)
        edge = NZ - 1 if backward else 0
        for d in far_first[::-1]:
            res_copy(k, b, d).wait_recv()
        landed(0, k, b)
        inner = NZ - 1 - edge
        total = resin[k, spot(k, b, inner), :]
        for s in range(NZ):
            if s != inner:
                total = total + times(resin[k, spot(k, b, s), :], maps[total_kind, s + (0 if backward else 1)])
        tin[k, x, at, :] = total
        for d in range(1, NX):
            t_copy(k, b, d).start()
        if b == 0:
            pass_on(0, k, 1)
        else:
            pass_on(1, k, 0)
        run = {}
        if backward:
            value = resin[k, spot(k, b, NZ - 1), :]
            run[NZ - 2] = value
            for s in range(NZ - 2, 0, -1):
                value = times(value, maps[chain_kind, s]) + resin[k, spot(k, b, s), :]
                run[s - 1] = value
        else:
            value = resin[k, spot(k, b, 0), :]
            run[1] = value
            for s in range(1, NZ - 1):
                value = times(value, maps[chain_kind, s]) + resin[k, spot(k, b, s), :]
                run[s + 1] = value
        for n in run:
            eout[k, spot(k, b, n), :] = run[n]
        if (k, b) == (0, 0):
            segments_arrive()
        for d in range(1, NX):
            t_copy(k, b, d).wait_recv()
        if backward:
            carry = jnp.where(x < NX - 1, tin[k, NX - 1, at, :], 0.0)
            for xs in range(NX - 2, 0, -1):
                carry = jnp.where(x < xs, times(carry, segs[1, xs]) + tin[k, xs, at, :], carry)
        else:
            carry = jnp.where(x > 0, tin[k, 0, at, :], 0.0)
            for xs in range(1, NX - 1):
                carry = jnp.where(x > xs, times(carry, segs[0, xs]) + tin[k, xs, at, :], carry)
        for n in range(NZ):
            if n == edge:
                eout[k, spot(k, b, n), :] = carry
            else:
                tile = maps[carry_kind, n + (1 if backward else 0)]
                eout[k, spot(k, b, n), :] = eout[k, spot(k, b, n), :] + times(carry, tile)
        hop(1, k, b)
        for d in far_first:
            e_copy(k, b, d).start()
        ein[k, spot(k, b, z), :] = eout[k, spot(k, b, z), :]

    def arrive(k, b):
        for d in far_first[::-1]:
            e_copy(k, b, d).wait_recv()
        landed(1, k, b)

    def relax(k, b, ahead, old):
        first, last = EDGES[k][b], EDGES[k][b + 1]
        lo = 0 if b == 0 else first + ahead
        hi = SIDE if b == BANDS - 1 else last + ahead
        for p, q in split(lo, hi):
            value = start[px(p, q), :] + STEP * conv(x3a, p, q, w[0])
            mid[px(p, q), :] = value
            fill(x3b, p, q, jnp.tanh(value))
        for p, q in split(first, last):
            value = mid[px(p, q), :] + STEP * conv(x3b, p, q, w[1])
            prop[px(p, q), :] = value
            resout[k, px(p, q), :] = value - old[px(p, q), :]
        if b == 0 and k > 0:
            pass_on(1, k - 1, 1)
        send_residual(k, b)
        if b == 1:
            pass_on(0, k, 0)


    relax(0, 0, 1, feat)

    def g_pass(d):
        g_copy(d).wait_recv()
        g_forward(d).start()

    each(NZ, g_pass, 1)
    for b in range(1, BANDS):
        relax(0, b, 1, feat)

    each(NZ, lambda d: g_forward(d).wait_recv(), 1)
    made, tiles = {}, {}

    def product(i, j):
        if (i, j) not in made:
            if i == j:
                value = gin[i]
            else:
                step = 1
                while (j // (2 * step)) * 2 * step > i:
                    step *= 2
                m = j // step * step
                value = times(product(i, m - 1), tile_of(m, j))
            made[i, j] = value
        return made[i, j]

    def tile_of(i, j):
        if (i, j) not in tiles:
            value = product(i, j)
            if i == j:
                put(maps, (0, i), value)
                tiles[i, j] = maps.at[0, i]
            elif j == NZ - 1:
                put(maps, (4, i), value)
                tiles[i, j] = maps.at[4, i]
            else:
                n = sum(i2 != j2 and j2 != NZ - 1 for i2, j2 in tiles)
                put(temps, (n,), value)
                tiles[i, j] = temps.at[n]
        return tiles[i, j][...]

    for n in range(NZ):
        tile_of(n, n)
    put(maps, (4, NZ), eye)
    put(maps, (4, NZ - 1), gin[NZ - 1])
    for n in range(NZ - 1):
        tile_of(n, NZ - 1)
    for n in range(NZ):
        prods[1, n] = product(n, NZ - 1)
        prods[0, n + 1] = product(0, n)
        put(maps, (2, n + 1), product(0, n))
    pin[x] = product(0, NZ - 1)

    def p_copy(d):
        return remote(pin.at[x], pin.at[x], p_s.at[d], p_r.at[d], to_x(d))

    each(NX, lambda d: p_copy(d).start(), 1)

    def segments_arrive():
        each(NX, lambda d: p_copy(d).wait_recv(), 1)
        for xs in range(1, NX - 1):
            put(segs, (0, xs), pin[xs])

    for b in range(BANDS):
        scan(0, b, False)

    def turn_kernels(layer):
        def turn(t):
            block = w[layer, pl.ds(pl.multiple_of((8 - t) * CH, CH), CH), :].astype(F32)
            wt[layer, pl.ds(pl.multiple_of(t * CH, CH), CH), :] = block.T.astype(BF16)
        each(9, turn)

    turn_kernels(1)
    turn_kernels(0)

    for b in range(BANDS):
        arrive(0, b)
        for p, q in split(EDGES[0][b], EDGES[0][b + 1]):
            e = ein[0, px(p, q), :]
            ends[px(p, q), :] = prop[px(p, q), :] + times(e, maps[0, z])
            value = start[px(p, q), :] + e
            start[px(p, q), :] = value
            fill(x3a, p, q, jnp.tanh(value))
        relax(1, b, 1, ends)

    loads[3].wait()
    for p, q in split(0, SIDE):
        fill(z3a, p, q, cot[px(p, q), :])
    for p, q in split(0, SIDE):
        ycot[px(p, q), :] = conv(z3a, p, q, wt[1])

    for b in range(BANDS):
        scan(1, b, False)

    def turn_maps(s):
        put(maps, (3, s + 1), prods[0, s + 1].T)

    put(maps, (3, 0), eye)
    each(NZ - 1, turn_maps)

    def pull(k, b, old):
        first, last = EDGES[k][b], EDGES[k][b + 1]
        for p, q in split(first, last):
            value = mid[px(p, q), :] + d0[px(p, q), :] * conv(z3b, p, q, wt[0])
            prop[px(p, q), :] = value
            resout[k, px(p, q), :] = value - old[px(p, q), :]
        if b == 0 and k > 0:
            pass_on(1, k - 1, 1)
        send_residual(k, b)
        if b == 1:
            pass_on(0, k, 0)

    def behind(k, b):
        lo = 0 if b == 0 else EDGES[k][b] + 1
        hi = SIDE if b == BANDS - 1 else EDGES[k][b + 1] + 1
        return split(lo, hi)

    for b in range(BANDS):
        arrive(1, b)
        for p, q in split(EDGES[1][b], EDGES[1][b + 1]):
            e = ein[1, px(p, q), :]
            ends[px(p, q), :] = prop[px(p, q), :] + times(e, maps[0, z])
            value = start[px(p, q), :] + e
            start[px(p, q), :] = value
            active = jnp.tanh(value)
            d0[px(p, q), :] = STEP * (1.0 - active * active)
            fill(x3a, p, q, active)
        for p, q in behind(2, b):
            active = jnp.tanh(start[px(p, q), :] + STEP * conv(x3a, p, q, w[0]))
            slope = STEP * (1.0 - active * active)
            d1[px(p, q), :] = slope
            fill(x3b, p, q, active)
            value = cot[px(p, q), :] + slope * ycot[px(p, q), :]
            mid[px(p, q), :] = value
            fill(z3b, p, q, value)
        pull(2, b, cot)

    def turn_more_maps(s):
        put(maps, (1, s), gin[s].T)
        put(maps, (5, s), prods[1, s].T)

    each(NZ, turn_more_maps)
    for xs in range(1, NX - 1):
        put(segs, (1, xs), pin[xs].T)

    for b in range(BANDS):
        scan(2, b, True)

    for b in range(BANDS):
        arrive(2, b)
        for p, q in split(EDGES[2][b], EDGES[2][b + 1]):
            f = ein[2, px(p, q), :]
            adj[px(p, q), :] = prop[px(p, q), :] + times(f, maps[1, z])
            value = cot[px(p, q), :] + f
            start[px(p, q), :] = value
            fill(z3a, p, q, value)
        for p, q in behind(3, b):
            value = start[px(p, q), :] + d1[px(p, q), :] * conv(z3a, p, q, wt[1])
            mid[px(p, q), :] = value
            fill(z3b, p, q, value)
        pull(3, b, adj)

    for b in range(BANDS):
        scan(3, b, True)

    def place(core, yy):
        return pl.ds(pl.multiple_of(core * half + yy * part, part), part)

    other = pl.ds(pl.multiple_of((NC - 1 - c) * half, half), half)

    def sib_copy(layer):
        return remote(local_grad.at[layer, other], gs.at[layer], sib_s.at[layer], sib_r.at[layer], to_core())

    def rs_copy(layer, d):
        return remote(hsum.at[layer, lax.rem(y + d, NY)], yin.at[layer, d], rs_s.at[layer, d], rs_r.at[layer, d], to_y(d))

    def ag_copy(layer, d):
        at = place(c, y)
        return remote(grad.at[layer, at], grad.at[layer, at], ag_s.at[layer, d], ag_r.at[layer, d], to_y(d))

    def fw_copy(layer, d):
        at = place(c, lax.rem(y + NY - d, NY))
        return remote(grad.at[layer, at], grad.at[layer, at], fw_s.at[layer, d], fw_r.at[layer, d], to_core())

    def reduce_core(layer):
        sib_copy(layer).wait()
        for yy in range(NY):
            hsum[layer, yy] = local_grad[layer, place(c, yy), :] + gs[layer, pl.ds(yy * part, part), :]
        each(NY, lambda d: rs_copy(layer, d).start(), 1)

    def reduce_chips(layer):
        total = hsum[layer, y]
        for d in range(1, NY):
            rs_copy(layer, d).wait_recv()
            total = total + yin[layer, d]
        grad[layer, place(c, y), :] = total * factor
        each(NY, lambda d: ag_copy(layer, d).start(), 1)
        fw_copy(layer, 0).start()

    def spread(layer):
        def go(d):
            ag_copy(layer, d).wait_recv()
            fw_copy(layer, d).start()
        each(NY, go, 1)

    def gradient(layer, signal, buffer, first, last, more):
        for r in range(3):
            block = jnp.dot(signal[:, px(first, last)], buffer[px(first + r, last + r), :], preferred_element_type=F32)
            for s in range(3):
                t = 3 * r + s
                value = block[:, CH * s : CH * (s + 1)].T
                at = slice(CH * t, CH * (t + 1))
                local_grad[layer, at, :] = local_grad[layer, at, :] + value if more else value

    def adjoint_out(b):
        for p, q in split(EDGES[3][b], EDGES[3][b + 1]):
            adj[px(p, q), :] = prop[px(p, q), :] + times(ein[3, px(p, q), :], maps[1, z])

    def top_signal(p, q):
        value = start[px(p, q), :] + ein[3, px(p, q), :]
        start[px(p, q), :] = value
        fill(z3a, p, q, value)
        zt[:, px(p, q)] = value.T.astype(BF16)

    def lower_signal(p, q):
        value = start[px(p, q), :] + d1[px(p, q), :] * conv(z3a, p, q, wt[1])
        zt0[:, px(p, q)] = value.T.astype(BF16)

    cut = EDGES[3][1] // 4 * 4
    low = (EDGES[3][1] - 1) // 4 * 4
    arrive(3, 0)
    pass_on(1, 3, 1)
    for p, q in split(0, cut, 8):
        top_signal(p, q)
    gradient(1, zt, x3b, 0, cut, False)
    for p, q in ((0, low // 8 * 4), (low // 8 * 4, low)):
        lower_signal(p, q)
    gradient(0, zt0, x3a, 0, low, False)
    adjoint_out(0)
    arrive(3, 1)
    for p, q in split(cut, SIDE, 8):
        top_signal(p, q)
    gradient(1, zt, x3b, cut, SIDE, True)
    sib_copy(1).start()
    for p, q in ((low, (low + SIDE) // 8 * 4), ((low + SIDE) // 8 * 4, SIDE)):
        lower_signal(p, q)
    gradient(0, zt0, x3a, low, SIDE, True)
    sib_copy(0).start()
    reduce_core(1)
    reduce_core(0)
    adjoint_out(1)
    reduce_chips(1)
    spread(1)
    reduce_chips(0)
    spread(0)
    for layer in range(2):
        each(NY, lambda d: fw_copy(layer, d).wait_recv(), 0)

    for layer in range(2):
        each(NY, lambda d: rs_copy(layer, d).wait_send(), 1)
        each(NY, lambda d: ag_copy(layer, d).wait_send(), 1)
        each(NY, lambda d: fw_copy(layer, d).wait_send(), 0)
    each(NZ, lambda d: g_copy(d).wait_send(), 1)
    each(NZ, lambda d: g_forward(d).wait_send(), 1)
    each(NX, lambda d: p_copy(d).wait_send(), 1)
    for k in range(4):
        for b in range(BANDS):
            for d in far_first:
                res_copy(k, b, d).wait_send()
                e_copy(k, b, d).wait_send()
            if opposite:
                for way in range(2):
                    for side in range(2):
                        hop_copy(way, k, b, side).wait_send()
                        land_copy(way, k, b, side).wait_send()
            each(NX, lambda d: t_copy(k, b, d).wait_send(), 1)


def make_local(NX, NZ, NY, NC):
    half = TAPS // NC
    part = half // NY
    dma = pltpu.SemaphoreType.DMA
    vmem = pltpu.VMEM
    image = vmem((PIXELS, CH), F32)
    padded = vmem((PIXELS + 2 * SIDE, 3 * CH), BF16)
    sweeps = vmem((4, PIXELS, CH), F32)
    moves = dma((4 * BANDS, NZ))

    def local(features, cotangent, weights, coarse_map):
        factor = STEP / (features.shape[0] * NY * NC)
        out = pl.pallas_call(
            functools.partial(body, NX, NZ, NY, NC, factor),
            out_shape=(
                jax.ShapeDtypeStruct((PIXELS, CH), F32),
                jax.ShapeDtypeStruct((PIXELS, CH), F32),
                jax.ShapeDtypeStruct((2, TAPS, CH), F32),
            ),
            in_specs=[pl.BlockSpec(memory_space=pl.ANY)] * 4,
            out_specs=[pl.BlockSpec(memory_space=vmem)] * 3,
            scratch_shapes=[
                image, image, vmem((2, TAPS, CH), BF16), vmem((CH, CH), F32),
                padded, padded, padded, padded,
                vmem((2, TAPS, CH), BF16),
                image, image, image, image, image, image,
                vmem((CH, PIXELS), BF16), vmem((CH, PIXELS), BF16),
                sweeps, sweeps, sweeps, sweeps,
                vmem((4, NX, PIXELS // NZ, CH), F32),
                vmem((NZ, CH, CH), F32),
                vmem((NX, CH, CH), F32),
                vmem((2, NZ + 1, CH, CH), F32),
                vmem((NZ, 2 * CH, 2 * CH), BF16),
                vmem((6, NZ + 1, 2 * CH, 2 * CH), BF16),
                vmem((2, NX, 2 * CH, 2 * CH), BF16),
                vmem((2, TAPS, CH), F32),
                vmem((2, half, CH), F32),
                vmem((2, NY, part, CH), F32),
                vmem((2, NY, part, CH), F32),
                dma((4,)),
                vmem((2, 4 * BANDS, 2, 48 * 8 // NZ, CH), F32),
                dma((2, 4 * BANDS, 2)), dma((2, 4 * BANDS, 2)), dma((2, 4 * BANDS, 2)), dma((2, 4 * BANDS, 2)),
                moves, moves, moves, moves, dma((4 * BANDS, NX)), dma((4 * BANDS, NX)),
                dma((NZ,)), dma((NZ,)), dma((NZ,)), dma((NZ,)), dma((NX,)), dma((NX,)),
                dma((2,)), dma((2,)), dma((2, NY)), dma((2, NY)), dma((2, NY)), dma((2, NY)), dma((2, NY)), dma((2, NY)),
            ],
            compiler_params=pltpu.CompilerParams(
                collective_id=0, has_side_effects=True, vmem_limit_bytes=40 * 1024 * 1024
            ),
            cost_estimate=pl.CostEstimate(flops=5 * 10**9, bytes_accessed=5 * 10**6, transcendentals=10**6),
        )(
            features.reshape(PIXELS, CH),
            cotangent.reshape(PIXELS, CH),
            weights.reshape(2, TAPS, CH),
            coarse_map.reshape(CH, CH),
        )
        shape = (1, 1, SIDE, SIDE, CH)
        return out[0].reshape(shape), out[1].reshape(shape), out[2].reshape(2, 9, CH, CH)

    return local


def build(mesh, sizes):
    return jax.shard_map(
        make_local(*sizes),
        mesh=mesh,
        in_specs=(P("dp", None, None, None), P("dp", None, None, None), P("tm", None, None, None), P("tm", None, None)),
        out_specs=(P("tm", "dp", None, None, None), P("tm", "dp", None, None, None), P("tm", None, None, None)),
        check_vma=False,
    )


def solution(mesh):
    return build(mesh, (4, 8, 4, 2))
```

```python
import functools

import jax
import jax.numpy as jnp
from jax import lax
from jax.experimental import pallas as pl
from jax.experimental.pallas import tpu as pltpu
from jax.sharding import PartitionSpec as P

MESH = pl.DeviceIdType.MESH
STEP = 0.25
DIAGONAL = 0.9
SIDE = 32
PIXELS = SIDE * SIDE
CH = 128
BANDS = 2
EDGES = ((0, 20, 32), (0, 18, 32), (0, 16, 32), (0, 14, 32))
TAPS = 9 * CH
F32, BF16 = jnp.float32, jnp.bfloat16


def two_terms(value):
    high = value.astype(BF16)
    return high, (value - high.astype(F32)).astype(BF16)


def times(value, tile):
    high, low = two_terms(value)
    both = jnp.dot(jnp.concatenate([high, low], 1), tile, preferred_element_type=F32)
    return both[:, :CH] + both[:, CH:]


def split(first, last, most=10):
    count = -(-(last - first) // most)
    cuts = [first + (last - first) * n // count for n in range(count + 1)]
    return list(zip(cuts[:-1], cuts[1:]))


def body(
    NX, NZ, NY, NC, factor,
    feat_in, cot_in, w_in, cm_in,
    ends, adj, grad,
    feat, cot, w, cm,
    x3a, x3b, z3a, z3b, wt, start, mid, prop, d0, d1, ycot, zt, zt0,
    resout, resin, eout, ein, tin, gin, pin, prods, temps, maps, segs, local_grad, gs, hsum, yin,
    in_s,
    res_s, res_r, e_s, e_r, t_s, t_r, g_s, g_r, gf_s, gf_r, p_s, p_r, sib_s, sib_r, rs_s, rs_r, ag_s, ag_r, fw_s, fw_r,
):
    loads = [
        pltpu.make_async_copy(src, dst, in_s.at[n])
        for n, (src, dst) in enumerate(((cm_in, cm), (feat_in, feat), (w_in, w), (cot_in, cot)))
    ]
    for load in loads:
        load.start()

    tm, dp = lax.axis_index("tm"), lax.axis_index("dp")
    x, z = tm // NZ, lax.rem(tm, NZ)
    y, c = dp // NC, lax.rem(dp, NC)
    half = TAPS // NC
    part = half // NY
    far_first = sorted(range(1, NZ), key=lambda d: -min(d, NZ - d))

    def to_z(d):
        return {"tm": x * NZ + lax.rem(z + d, NZ)}

    def to_x(d):
        return {"tm": lax.rem(x + d, NX) * NZ + z}

    def to_y(d):
        return {"dp": lax.rem(y + d, NY) * NC + c}

    def to_core():
        return {"dp": y * NC + (NC - 1 - c)}

    def remote(src, dst, send, recv, device):
        return pltpu.make_async_remote_copy(
            src_ref=src, dst_ref=dst, send_sem=send, recv_sem=recv, device_id=device, device_id_type=MESH
        )

    def each(count, f, first=0):
        def go(i, carry):
            f(i)
            return carry
        lax.fori_loop(first, count, go, 0)

    barrier = pltpu.get_barrier_semaphore()

    def greet(device):
        pl.semaphore_signal(barrier, inc=1, device_id=device, device_id_type=MESH)

    each(NZ, lambda d: greet(to_z(d)), 1)
    each(NX, lambda d: greet(to_x(d)), 1)
    each(NY, lambda d: greet(to_y(d)), 1)
    greet(to_core())

    def px(first, last):
        return slice(first * SIDE, last * SIDE)

    def fill(buffer, first, last, value):
        size = (last - first) * SIDE
        column = lax.rem(lax.broadcasted_iota(jnp.int32, (size, CH), 0), SIDE)
        left = jnp.where(column == 0, 0.0, pltpu.roll(value, 1, 0))
        right = jnp.where(column == SIDE - 1, 0.0, pltpu.roll(value, size - 1, 0))
        at = px(first + 1, last + 1)
        buffer[at, :CH] = left.astype(BF16)
        buffer[at, CH : 2 * CH] = value.astype(BF16)
        buffer[at, 2 * CH :] = right.astype(BF16)

    def conv(buffer, first, last, kernel):
        pieces = [buffer[px(first + r, last + r), :] for r in range(3)]
        return jnp.dot(jnp.concatenate(pieces, 1), kernel, preferred_element_type=F32)

    zero_row = jnp.zeros((SIDE, 3 * CH), BF16)
    for buffer in (x3a, x3b, z3a, z3b):
        buffer[:SIDE, :] = zero_row
        buffer[PIXELS + SIDE :, :] = zero_row
    eye = (lax.broadcasted_iota(jnp.int32, (CH, CH), 0) == lax.broadcasted_iota(jnp.int32, (CH, CH), 1)).astype(F32)
    loads[0].wait()
    gin[z] = DIAGONAL * eye + cm[...]

    loads[1].wait()
    for p, q in split(0, SIDE):
        value = feat[px(p, q), :]
        start[px(p, q), :] = value
        fill(x3a, p, q, jnp.tanh(value))
    loads[2].wait()
    pl.semaphore_wait(barrier, NZ - 1 + NX - 1 + NY - 1 + 1)

    gh = pl.ds(pl.multiple_of(c * (CH // NC), CH // NC), CH // NC)

    def g_copy(d):
        return remote(gin.at[z, gh], gin.at[z, gh], g_s.at[d], g_r.at[d], to_z(d))

    def g_forward(d):
        zs = lax.rem(z + NZ - d, NZ)
        return remote(gin.at[zs, gh], gin.at[zs, gh], gf_s.at[d], gf_r.at[d], to_core())

    for d in far_first:
        g_copy(d).start()

    def share(k, b):
        first, last = EDGES[k][b], EDGES[k][b + 1]
        return first * SIDE, (last - first) * SIDE // NZ

    def spot(k, b, n):
        base, R = share(k, b)
        if isinstance(n, int):
            return slice(base + n * R, base + n * R + R)
        return pl.ds(pl.multiple_of(base + n * R, 8), R)

    def res_copy(k, b, d):
        zp = lax.rem(z + d, NZ)
        m = BANDS * k + b
        return remote(
            resout.at[k, spot(k, b, zp)], resin.at[k, spot(k, b, z)], res_s.at[m, d], res_r.at[m, d], to_z(d)
        )

    def send_residual(k, b):
        for d in far_first:
            res_copy(k, b, d).start()
        resin[k, spot(k, b, z), :] = resout[k, spot(k, b, z), :]

    def t_spot(k, b):
        base, R = share(k, b)
        return slice(base // NZ, base // NZ + R)

    def t_copy(k, b, d):
        m = BANDS * k + b
        at = t_spot(k, b)
        return remote(tin.at[k, x, at], tin.at[k, x, at], t_s.at[m, d], t_r.at[m, d], to_x(d))

    def e_copy(k, b, d):
        zp = lax.rem(z + d, NZ)
        m = BANDS * k + b
        return remote(eout.at[k, spot(k, b, zp)], ein.at[k, spot(k, b, z)], e_s.at[m, d], e_r.at[m, d], to_z(d))

    def put(where, index, matrix):
        high, low = two_terms(matrix)
        where[(*index, slice(0, CH), slice(0, CH))] = high
        where[(*index, slice(0, CH), slice(CH, None))] = low
        where[(*index, slice(CH, None), slice(0, CH))] = high
        where[(*index, slice(CH, None), slice(CH, None))] = jnp.zeros((CH, CH), BF16)

    def sent(k, b):
        for d in far_first:
            res_copy(k, b, d).wait_send()
            e_copy(k, b, d).wait_send()
        for d in range(1, NX):
            t_copy(k, b, d).wait_send()

    def scan(k, b, backward, meanwhile=None):
        total_kind, chain_kind, carry_kind = (3, 1, 5) if backward else (4, 0, 2)
        at = t_spot(k, b)
        edge = NZ - 1 if backward else 0

        def term(d):
            s = lax.rem(z + NZ - d, NZ)
            return times(resin[k, spot(k, b, s), :], maps[total_kind, s + (0 if backward else 1)])

        near = far_first[::-1][: NZ // 2]
        for d in near:
            res_copy(k, b, d).wait_recv()
        total = term(0)
        for d in near:
            total = total + term(d)
        for d in far_first[::-1][NZ // 2 :]:
            res_copy(k, b, d).wait_recv()
        for d in far_first[::-1][NZ // 2 :]:
            total = total + term(d)
        tin[k, x, at, :] = total
        for d in range(1, NX):
            t_copy(k, b, d).start()
        run = {}
        if backward:
            value = resin[k, spot(k, b, NZ - 1), :]
            run[NZ - 2] = value
            for s in range(NZ - 2, 0, -1):
                value = times(value, maps[chain_kind, s]) + resin[k, spot(k, b, s), :]
                run[s - 1] = value
        else:
            value = resin[k, spot(k, b, 0), :]
            run[1] = value
            for s in range(1, NZ - 1):
                value = times(value, maps[chain_kind, s]) + resin[k, spot(k, b, s), :]
                run[s + 1] = value
        for n in run:
            eout[k, spot(k, b, n), :] = run[n]
        if meanwhile is not None:
            meanwhile()
        if k > 0:
            sent(k - 1, b)
        for d in range(1, NX):
            t_copy(k, b, d).wait_recv()
        if backward:
            carry = jnp.where(x < NX - 1, tin[k, NX - 1, at, :], 0.0)
            for xs in range(NX - 2, 0, -1):
                carry = jnp.where(x < xs, times(carry, segs[1, xs]) + tin[k, xs, at, :], carry)
        else:
            carry = jnp.where(x > 0, tin[k, 0, at, :], 0.0)
            for xs in range(1, NX - 1):
                carry = jnp.where(x > xs, times(carry, segs[0, xs]) + tin[k, xs, at, :], carry)
        for n in range(NZ):
            if n == edge:
                eout[k, spot(k, b, n), :] = carry
            else:
                tile = maps[carry_kind, n + (1 if backward else 0)]
                eout[k, spot(k, b, n), :] = eout[k, spot(k, b, n), :] + times(carry, tile)
        for d in far_first:
            e_copy(k, b, d).start()
        ein[k, spot(k, b, z), :] = eout[k, spot(k, b, z), :]

    def arrive(k, b):
        for d in far_first[::-1]:
            e_copy(k, b, d).wait_recv()

    def relax(k, b, ahead, old):
        first, last = EDGES[k][b], EDGES[k][b + 1]
        lo = 0 if b == 0 else first + ahead
        hi = SIDE if b == BANDS - 1 else last + ahead
        for p, q in split(lo, hi):
            value = start[px(p, q), :] + STEP * conv(x3a, p, q, w[0])
            mid[px(p, q), :] = value
            fill(x3b, p, q, jnp.tanh(value))
        for p, q in split(first, last):
            value = mid[px(p, q), :] + STEP * conv(x3b, p, q, w[1])
            prop[px(p, q), :] = value
            resout[k, px(p, q), :] = value - old[px(p, q), :]
        send_residual(k, b)


    relax(0, 0, 1, feat)

    def g_pass(d):
        g_copy(d).wait_recv()
        g_forward(d).start()

    each(NZ, g_pass, 1)
    for b in range(1, BANDS):
        relax(0, b, 1, feat)

    each(NZ, lambda d: g_forward(d).wait_recv(), 1)
    made, tiles = {}, {}

    def product(i, j):
        if (i, j) not in made:
            if i == j:
                value = gin[i]
            else:
                step = 1
                while (j // (2 * step)) * 2 * step > i:
                    step *= 2
                m = j // step * step
                value = times(product(i, m - 1), tile_of(m, j))
            made[i, j] = value
        return made[i, j]

    def tile_of(i, j):
        if (i, j) not in tiles:
            value = product(i, j)
            if i == j:
                put(maps, (0, i), value)
                tiles[i, j] = maps.at[0, i]
            elif j == NZ - 1:
                put(maps, (4, i), value)
                tiles[i, j] = maps.at[4, i]
            else:
                n = sum(i2 != j2 and j2 != NZ - 1 for i2, j2 in tiles)
                put(temps, (n,), value)
                tiles[i, j] = temps.at[n]
        return tiles[i, j][...]

    for n in range(NZ):
        tile_of(n, n)
    put(maps, (4, NZ), eye)
    put(maps, (4, NZ - 1), gin[NZ - 1])
    for n in range(NZ - 1):
        tile_of(n, NZ - 1)
    for n in range(NZ):
        prods[1, n] = product(n, NZ - 1)
        prods[0, n + 1] = product(0, n)
        put(maps, (2, n + 1), product(0, n))
    pin[x] = product(0, NZ - 1)

    def p_copy(d):
        return remote(pin.at[x], pin.at[x], p_s.at[d], p_r.at[d], to_x(d))

    each(NX, lambda d: p_copy(d).start(), 1)

    def segments_arrive():
        each(NX, lambda d: p_copy(d).wait_recv(), 1)
        for xs in range(1, NX - 1):
            put(segs, (0, xs), pin[xs])

    def turn_kernels(layer):
        def turn(t):
            block = w[layer, pl.ds(pl.multiple_of((8 - t) * CH, CH), CH), :].astype(F32)
            wt[layer, pl.ds(pl.multiple_of(t * CH, CH), CH), :] = block.T.astype(BF16)
        each(9, turn)

    def first_slot():
        segments_arrive()
        turn_kernels(1)

    for b in range(BANDS):
        scan(0, b, False, (first_slot, lambda: turn_kernels(0), None)[b])

    for b in range(BANDS):
        arrive(0, b)
        for p, q in split(EDGES[0][b], EDGES[0][b + 1]):
            e = ein[0, px(p, q), :]
            ends[px(p, q), :] = prop[px(p, q), :] + times(e, maps[0, z])
            value = start[px(p, q), :] + e
            start[px(p, q), :] = value
            fill(x3a, p, q, jnp.tanh(value))
        relax(1, b, 1, ends)

    def turn_maps(s):
        put(maps, (3, s + 1), prods[0, s + 1].T)

    def second_slot():
        put(maps, (3, 0), eye)
        each(NZ - 1, turn_maps)

    def third_slot():
        loads[3].wait()
        for p, q in split(0, SIDE):
            fill(z3a, p, q, cot[px(p, q), :])
        for p, q in split(0, SIDE):
            ycot[px(p, q), :] = conv(z3a, p, q, wt[1])

    for b in range(BANDS):
        scan(1, b, False, (second_slot, third_slot, None)[b])

    def pull(k, b, old):
        first, last = EDGES[k][b], EDGES[k][b + 1]
        for p, q in split(first, last):
            value = mid[px(p, q), :] + d0[px(p, q), :] * conv(z3b, p, q, wt[0])
            prop[px(p, q), :] = value
            resout[k, px(p, q), :] = value - old[px(p, q), :]
        send_residual(k, b)

    def behind(k, b):
        lo = 0 if b == 0 else EDGES[k][b] + 1
        hi = SIDE if b == BANDS - 1 else EDGES[k][b + 1] + 1
        return split(lo, hi)

    for b in range(BANDS):
        arrive(1, b)
        for p, q in split(EDGES[1][b], EDGES[1][b + 1]):
            e = ein[1, px(p, q), :]
            ends[px(p, q), :] = prop[px(p, q), :] + times(e, maps[0, z])
            value = start[px(p, q), :] + e
            start[px(p, q), :] = value
            active = jnp.tanh(value)
            d0[px(p, q), :] = STEP * (1.0 - active * active)
            fill(x3a, p, q, active)
        for p, q in behind(2, b):
            active = jnp.tanh(start[px(p, q), :] + STEP * conv(x3a, p, q, w[0]))
            slope = STEP * (1.0 - active * active)
            d1[px(p, q), :] = slope
            fill(x3b, p, q, active)
            value = cot[px(p, q), :] + slope * ycot[px(p, q), :]
            mid[px(p, q), :] = value
            fill(z3b, p, q, value)
        pull(2, b, cot)

    def turn_steps(s):
        put(maps, (1, s), gin[s].T)

    def turn_carries(s):
        put(maps, (5, s), prods[1, s].T)

    def fourth_slot():
        each(NZ, turn_carries)
        each(NZ, lambda d: g_copy(d).wait_send(), 1)
        each(NZ, lambda d: g_forward(d).wait_send(), 1)
        each(NX, lambda d: p_copy(d).wait_send(), 1)
        for xs in range(1, NX - 1):
            put(segs, (1, xs), pin[xs].T)

    each(NZ, turn_steps)
    for b in range(BANDS):
        scan(2, b, True, (fourth_slot, None, None)[b])

    for b in range(BANDS):
        arrive(2, b)
        for p, q in split(EDGES[2][b], EDGES[2][b + 1]):
            f = ein[2, px(p, q), :]
            adj[px(p, q), :] = prop[px(p, q), :] + times(f, maps[1, z])
            value = cot[px(p, q), :] + f
            start[px(p, q), :] = value
            fill(z3a, p, q, value)
        for p, q in behind(3, b):
            value = start[px(p, q), :] + d1[px(p, q), :] * conv(z3a, p, q, wt[1])
            mid[px(p, q), :] = value
            fill(z3b, p, q, value)
        pull(3, b, adj)

    for b in range(BANDS):
        scan(3, b, True)

    def place(core, yy):
        return pl.ds(pl.multiple_of(core * half + yy * part, part), part)

    other = pl.ds(pl.multiple_of((NC - 1 - c) * half, half), half)

    def sib_copy(layer):
        return remote(local_grad.at[layer, other], gs.at[layer], sib_s.at[layer], sib_r.at[layer], to_core())

    def rs_copy(layer, d):
        return remote(hsum.at[layer, lax.rem(y + d, NY)], yin.at[layer, d], rs_s.at[layer, d], rs_r.at[layer, d], to_y(d))

    def ag_copy(layer, d):
        at = place(c, y)
        return remote(grad.at[layer, at], grad.at[layer, at], ag_s.at[layer, d], ag_r.at[layer, d], to_y(d))

    def fw_copy(layer, d):
        at = place(c, lax.rem(y + NY - d, NY))
        return remote(grad.at[layer, at], grad.at[layer, at], fw_s.at[layer, d], fw_r.at[layer, d], to_core())

    def reduce_core(layer):
        sib_copy(layer).wait()
        for yy in range(NY):
            hsum[layer, yy] = local_grad[layer, place(c, yy), :] + gs[layer, pl.ds(yy * part, part), :]
        each(NY, lambda d: rs_copy(layer, d).start(), 1)

    def reduce_chips(layer):
        total = hsum[layer, y]
        for d in range(1, NY):
            rs_copy(layer, d).wait_recv()
            total = total + yin[layer, d]
        grad[layer, place(c, y), :] = total * factor
        each(NY, lambda d: ag_copy(layer, d).start(), 1)
        fw_copy(layer, 0).start()

    def spread(layer):
        def go(d):
            ag_copy(layer, d).wait_recv()
            fw_copy(layer, d).start()
        each(NY, go, 1)

    def gradient(layer, signal, buffer, first, last, more):
        for r in range(3):
            block = jnp.dot(signal[:, px(first, last)], buffer[px(first + r, last + r), :], preferred_element_type=F32)
            for s in range(3):
                t = 3 * r + s
                value = block[:, CH * s : CH * (s + 1)].T
                at = slice(CH * t, CH * (t + 1))
                local_grad[layer, at, :] = local_grad[layer, at, :] + value if more else value

    def adjoint_out(b):
        for p, q in split(EDGES[3][b], EDGES[3][b + 1]):
            adj[px(p, q), :] = prop[px(p, q), :] + times(ein[3, px(p, q), :], maps[1, z])

    def top_signal(p, q):
        value = start[px(p, q), :] + ein[3, px(p, q), :]
        start[px(p, q), :] = value
        fill(z3a, p, q, value)
        zt[:, px(p, q)] = value.T.astype(BF16)

    def lower_signal(p, q):
        value = start[px(p, q), :] + d1[px(p, q), :] * conv(z3a, p, q, wt[1])
        zt0[:, px(p, q)] = value.T.astype(BF16)

    cuts = [e // 4 * 4 for e in EDGES[3]]
    lows = [0] + [(e - 1) // 4 * 4 for e in cuts[1:-1]] + [SIDE]

    def halves(first, last):
        middle = (first + last) // 8 * 4
        return [(p, q) for p, q in ((first, middle), (middle, last)) if q > p]

    for b in range(BANDS):
        arrive(3, b)
        for p, q in halves(cuts[b], cuts[b + 1]):
            top_signal(p, q)
        gradient(1, zt, x3b, cuts[b], cuts[b + 1], b > 0)
        if b == BANDS - 1:
            sib_copy(1).start()
        for p, q in halves(lows[b], lows[b + 1]):
            lower_signal(p, q)
        if b == BANDS - 1:
            reduce_core(1)
        gradient(0, zt0, x3a, lows[b], lows[b + 1], b > 0)
        if b < BANDS - 1:
            adjoint_out(b)
    sib_copy(0).start()
    adjoint_out(BANDS - 1)
    reduce_core(0)
    reduce_chips(1)
    reduce_chips(0)
    for b in range(BANDS):
        sent(3, b)
    spread(1)
    spread(0)
    for layer in range(2):
        each(NY, lambda d: fw_copy(layer, d).wait_recv(), 0)

    for layer in range(2):
        each(NY, lambda d: rs_copy(layer, d).wait_send(), 1)
        each(NY, lambda d: ag_copy(layer, d).wait_send(), 1)
        each(NY, lambda d: fw_copy(layer, d).wait_send(), 0)


def make_local(NX, NZ, NY, NC):
    half = TAPS // NC
    part = half // NY
    dma = pltpu.SemaphoreType.DMA
    vmem = pltpu.VMEM
    image = vmem((PIXELS, CH), F32)
    padded = vmem((PIXELS + 2 * SIDE, 3 * CH), BF16)
    sweeps = vmem((4, PIXELS, CH), F32)
    moves = dma((4 * BANDS, NZ))

    def local(features, cotangent, weights, coarse_map):
        factor = STEP / (features.shape[0] * NY * NC)
        out = pl.pallas_call(
            functools.partial(body, NX, NZ, NY, NC, factor),
            out_shape=(
                jax.ShapeDtypeStruct((PIXELS, CH), F32),
                jax.ShapeDtypeStruct((PIXELS, CH), F32),
                jax.ShapeDtypeStruct((2, TAPS, CH), F32),
            ),
            in_specs=[pl.BlockSpec(memory_space=pltpu.HBM)] * 4,
            out_specs=[pl.BlockSpec(memory_space=vmem)] * 3,
            scratch_shapes=[
                image, image, vmem((2, TAPS, CH), BF16), vmem((CH, CH), F32),
                padded, padded, padded, padded,
                vmem((2, TAPS, CH), BF16),
                image, image, image, image, image, image,
                vmem((CH, PIXELS), BF16), vmem((CH, PIXELS), BF16),
                sweeps, sweeps, sweeps, sweeps,
                vmem((4, NX, PIXELS // NZ, CH), F32),
                vmem((NZ, CH, CH), F32),
                vmem((NX, CH, CH), F32),
                vmem((2, NZ + 1, CH, CH), F32),
                vmem((NZ, 2 * CH, 2 * CH), BF16),
                vmem((6, NZ + 1, 2 * CH, 2 * CH), BF16),
                vmem((2, NX, 2 * CH, 2 * CH), BF16),
                vmem((2, TAPS, CH), F32),
                vmem((2, half, CH), F32),
                vmem((2, NY, part, CH), F32),
                vmem((2, NY, part, CH), F32),
                dma((4,)),
                moves, moves, moves, moves, dma((4 * BANDS, NX)), dma((4 * BANDS, NX)),
                dma((NZ,)), dma((NZ,)), dma((NZ,)), dma((NZ,)), dma((NX,)), dma((NX,)),
                dma((2,)), dma((2,)), dma((2, NY)), dma((2, NY)), dma((2, NY)), dma((2, NY)), dma((2, NY)), dma((2, NY)),
            ],
            compiler_params=pltpu.CompilerParams(
                collective_id=0, has_side_effects=True, vmem_limit_bytes=48 * 1024 * 1024
            ),
            cost_estimate=pl.CostEstimate(flops=5 * 10**9, bytes_accessed=5 * 10**6, transcendentals=10**6),
        )(
            features.reshape(PIXELS, CH),
            cotangent.reshape(PIXELS, CH),
            weights.reshape(2, TAPS, CH),
            coarse_map.reshape(CH, CH),
        )
        shape = (1, 1, SIDE, SIDE, CH)
        return out[0].reshape(shape), out[1].reshape(shape), out[2].reshape(2, 9, CH, CH)

    return local


def build(mesh, sizes):
    return jax.shard_map(
        make_local(*sizes),
        mesh=mesh,
        in_specs=(P("dp", None, None, None), P("dp", None, None, None), P("tm", None, None, None), P("tm", None, None)),
        out_specs=(P("tm", "dp", None, None, None), P("tm", "dp", None, None, None), P("tm", None, None, None)),
        check_vma=False,
    )


def solution(mesh):
    return build(mesh, (4, 8, 4, 2))
```

```python
import functools

import jax
import jax.numpy as jnp
from jax import lax
from jax.experimental import pallas as pl
from jax.experimental.pallas import tpu as pltpu
from jax.sharding import PartitionSpec as P

MESH = pl.DeviceIdType.MESH
STEP = 0.25
DIAGONAL = 0.9
SIDE = 32
PIXELS = SIDE * SIDE
CH = 128
BANDS = 3
EDGES = ((0, 14, 24, 32), (0, 12, 22, 32), (0, 10, 20, 32), (0, 8, 18, 32))
TAPS = 9 * CH
F32, BF16 = jnp.float32, jnp.bfloat16


def two_terms(value):
    high = value.astype(BF16)
    return high, (value - high.astype(F32)).astype(BF16)


def times(value, tile):
    high, low = two_terms(value)
    both = jnp.dot(jnp.concatenate([high, low], 1), tile, preferred_element_type=F32)
    return both[:, :CH] + both[:, CH:]


def split(first, last, most=10):
    count = -(-(last - first) // most)
    cuts = [first + (last - first) * n // count for n in range(count + 1)]
    return list(zip(cuts[:-1], cuts[1:]))


def body(
    NX, NZ, NY, NC, factor,
    feat_in, cot_in, w_in, cm_in,
    ends, adj, grad,
    feat, cot, w, cm,
    x3a, x3b, z3a, z3b, wt, start, mid, prop, d0, d1, ycot, zt, zt0,
    resout, resin, eout, ein, tin, gin, pin, prods, temps, maps, segs, local_grad, gs, hsum, yin,
    in_s,
    res_s, res_r, e_s, e_r, t_s, t_r, g_s, g_r, gf_s, gf_r, p_s, p_r, sib_s, sib_r, rs_s, rs_r, ag_s, ag_r, fw_s, fw_r,
):
    loads = [
        pltpu.make_async_copy(src, dst, in_s.at[n])
        for n, (src, dst) in enumerate(((cm_in, cm), (feat_in, feat), (w_in, w), (cot_in, cot)))
    ]
    for load in loads:
        load.start()

    tm, dp = lax.axis_index("tm"), lax.axis_index("dp")
    x, z = tm // NZ, lax.rem(tm, NZ)
    y, c = dp // NC, lax.rem(dp, NC)
    half = TAPS // NC
    part = half // NY
    far_first = sorted(range(1, NZ), key=lambda d: -min(d, NZ - d))

    def to_z(d):
        return {"tm": x * NZ + lax.rem(z + d, NZ)}

    def to_x(d):
        return {"tm": lax.rem(x + d, NX) * NZ + z}

    def to_y(d):
        return {"dp": lax.rem(y + d, NY) * NC + c}

    def to_core():
        return {"dp": y * NC + (NC - 1 - c)}

    def remote(src, dst, send, recv, device):
        return pltpu.make_async_remote_copy(
            src_ref=src, dst_ref=dst, send_sem=send, recv_sem=recv, device_id=device, device_id_type=MESH
        )

    def each(count, f, first=0):
        def go(i, carry):
            f(i)
            return carry
        lax.fori_loop(first, count, go, 0)

    barrier = pltpu.get_barrier_semaphore()

    def greet(device):
        pl.semaphore_signal(barrier, inc=1, device_id=device, device_id_type=MESH)

    each(NZ, lambda d: greet(to_z(d)), 1)
    each(NX, lambda d: greet(to_x(d)), 1)
    each(NY, lambda d: greet(to_y(d)), 1)
    greet(to_core())

    def px(first, last):
        return slice(first * SIDE, last * SIDE)

    def fill(buffer, first, last, value):
        size = (last - first) * SIDE
        column = lax.rem(lax.broadcasted_iota(jnp.int32, (size, CH), 0), SIDE)
        left = jnp.where(column == 0, 0.0, pltpu.roll(value, 1, 0))
        right = jnp.where(column == SIDE - 1, 0.0, pltpu.roll(value, size - 1, 0))
        at = px(first + 1, last + 1)
        buffer[at, :CH] = left.astype(BF16)
        buffer[at, CH : 2 * CH] = value.astype(BF16)
        buffer[at, 2 * CH :] = right.astype(BF16)

    def conv(buffer, first, last, kernel):
        pieces = [buffer[px(first + r, last + r), :] for r in range(3)]
        return jnp.dot(jnp.concatenate(pieces, 1), kernel, preferred_element_type=F32)

    zero_row = jnp.zeros((SIDE, 3 * CH), BF16)
    for buffer in (x3a, x3b, z3a, z3b):
        buffer[:SIDE, :] = zero_row
        buffer[PIXELS + SIDE :, :] = zero_row
    eye = (lax.broadcasted_iota(jnp.int32, (CH, CH), 0) == lax.broadcasted_iota(jnp.int32, (CH, CH), 1)).astype(F32)
    loads[0].wait()
    gin[z] = DIAGONAL * eye + cm[...]

    loads[1].wait()
    for p, q in split(0, SIDE):
        value = feat[px(p, q), :]
        start[px(p, q), :] = value
        fill(x3a, p, q, jnp.tanh(value))
    loads[2].wait()
    pl.semaphore_wait(barrier, NZ - 1 + NX - 1 + NY - 1 + 1)

    gh = pl.ds(pl.multiple_of(c * (CH // NC), CH // NC), CH // NC)

    def g_copy(d):
        return remote(gin.at[z, gh], gin.at[z, gh], g_s.at[d], g_r.at[d], to_z(d))

    def g_forward(d):
        zs = lax.rem(z + NZ - d, NZ)
        return remote(gin.at[zs, gh], gin.at[zs, gh], gf_s.at[d], gf_r.at[d], to_core())

    for d in far_first:
        g_copy(d).start()

    def share(k, b):
        first, last = EDGES[k][b], EDGES[k][b + 1]
        return first * SIDE, (last - first) * SIDE // NZ

    def spot(k, b, n):
        base, R = share(k, b)
        if isinstance(n, int):
            return slice(base + n * R, base + n * R + R)
        return pl.ds(pl.multiple_of(base + n * R, 8), R)

    def res_copy(k, b, d):
        zp = lax.rem(z + d, NZ)
        m = BANDS * k + b
        return remote(
            resout.at[k, spot(k, b, zp)], resin.at[k, spot(k, b, z)], res_s.at[m, d], res_r.at[m, d], to_z(d)
        )

    def send_residual(k, b):
        for d in far_first:
            res_copy(k, b, d).start()
        resin[k, spot(k, b, z), :] = resout[k, spot(k, b, z), :]

    def t_spot(k, b):
        base, R = share(k, b)
        return slice(base // NZ, base // NZ + R)

    def t_copy(k, b, d):
        m = BANDS * k + b
        at = t_spot(k, b)
        return remote(tin.at[k, x, at], tin.at[k, x, at], t_s.at[m, d], t_r.at[m, d], to_x(d))

    def e_copy(k, b, d):
        zp = lax.rem(z + d, NZ)
        m = BANDS * k + b
        return remote(eout.at[k, spot(k, b, zp)], ein.at[k, spot(k, b, z)], e_s.at[m, d], e_r.at[m, d], to_z(d))

    def put(where, index, matrix):
        high, low = two_terms(matrix)
        where[(*index, slice(0, CH), slice(0, CH))] = high
        where[(*index, slice(0, CH), slice(CH, None))] = low
        where[(*index, slice(CH, None), slice(0, CH))] = high
        where[(*index, slice(CH, None), slice(CH, None))] = jnp.zeros((CH, CH), BF16)

    def sent(k, b):
        for d in far_first:
            res_copy(k, b, d).wait_send()
            e_copy(k, b, d).wait_send()
        for d in range(1, NX):
            t_copy(k, b, d).wait_send()

    def scan(k, b, backward, meanwhile=None):
        total_kind, chain_kind, carry_kind = (3, 1, 5) if backward else (4, 0, 2)
        at = t_spot(k, b)
        edge = NZ - 1 if backward else 0

        def term(d):
            s = lax.rem(z + NZ - d, NZ)
            return times(resin[k, spot(k, b, s), :], maps[total_kind, s + (0 if backward else 1)])

        near = far_first[::-1][: NZ // 2]
        for d in near:
            res_copy(k, b, d).wait_recv()
        total = term(0)
        for d in near:
            total = total + term(d)
        for d in far_first[::-1][NZ // 2 :]:
            res_copy(k, b, d).wait_recv()
        for d in far_first[::-1][NZ // 2 :]:
            total = total + term(d)
        tin[k, x, at, :] = total
        for d in range(1, NX):
            t_copy(k, b, d).start()
        run = {}
        if backward:
            value = resin[k, spot(k, b, NZ - 1), :]
            run[NZ - 2] = value
            for s in range(NZ - 2, 0, -1):
                value = times(value, maps[chain_kind, s]) + resin[k, spot(k, b, s), :]
                run[s - 1] = value
        else:
            value = resin[k, spot(k, b, 0), :]
            run[1] = value
            for s in range(1, NZ - 1):
                value = times(value, maps[chain_kind, s]) + resin[k, spot(k, b, s), :]
                run[s + 1] = value
        for n in run:
            eout[k, spot(k, b, n), :] = run[n]
        if meanwhile is not None:
            meanwhile()
        if k > 0:
            sent(k - 1, b)
        for d in range(1, NX):
            t_copy(k, b, d).wait_recv()
        if backward:
            carry = jnp.where(x < NX - 1, tin[k, NX - 1, at, :], 0.0)
            for xs in range(NX - 2, 0, -1):
                carry = jnp.where(x < xs, times(carry, segs[1, xs]) + tin[k, xs, at, :], carry)
        else:
            carry = jnp.where(x > 0, tin[k, 0, at, :], 0.0)
            for xs in range(1, NX - 1):
                carry = jnp.where(x > xs, times(carry, segs[0, xs]) + tin[k, xs, at, :], carry)
        for n in range(NZ):
            if n == edge:
                eout[k, spot(k, b, n), :] = carry
            else:
                tile = maps[carry_kind, n + (1 if backward else 0)]
                eout[k, spot(k, b, n), :] = eout[k, spot(k, b, n), :] + times(carry, tile)
        for d in far_first:
            e_copy(k, b, d).start()
        ein[k, spot(k, b, z), :] = eout[k, spot(k, b, z), :]

    def arrive(k, b):
        for d in far_first[::-1]:
            e_copy(k, b, d).wait_recv()

    def relax(k, b, ahead, old):
        first, last = EDGES[k][b], EDGES[k][b + 1]
        lo = 0 if b == 0 else first + ahead
        hi = SIDE if b == BANDS - 1 else last + ahead
        for p, q in split(lo, hi):
            value = start[px(p, q), :] + STEP * conv(x3a, p, q, w[0])
            mid[px(p, q), :] = value
            fill(x3b, p, q, jnp.tanh(value))
        for p, q in split(first, last):
            value = mid[px(p, q), :] + STEP * conv(x3b, p, q, w[1])
            prop[px(p, q), :] = value
            resout[k, px(p, q), :] = value - old[px(p, q), :]
        send_residual(k, b)


    relax(0, 0, 1, feat)

    def g_pass(d):
        g_copy(d).wait_recv()
        g_forward(d).start()

    each(NZ, g_pass, 1)
    for b in range(1, BANDS):
        relax(0, b, 1, feat)

    each(NZ, lambda d: g_forward(d).wait_recv(), 1)
    made, tiles = {}, {}

    def product(i, j):
        if (i, j) not in made:
            if i == j:
                value = gin[i]
            else:
                step = 1
                while (j // (2 * step)) * 2 * step > i:
                    step *= 2
                m = j // step * step
                value = times(product(i, m - 1), tile_of(m, j))
            made[i, j] = value
        return made[i, j]

    def tile_of(i, j):
        if (i, j) not in tiles:
            value = product(i, j)
            if i == j:
                put(maps, (0, i), value)
                tiles[i, j] = maps.at[0, i]
            elif j == NZ - 1:
                put(maps, (4, i), value)
                tiles[i, j] = maps.at[4, i]
            else:
                n = sum(i2 != j2 and j2 != NZ - 1 for i2, j2 in tiles)
                put(temps, (n,), value)
                tiles[i, j] = temps.at[n]
        return tiles[i, j][...]

    for n in range(NZ):
        tile_of(n, n)
    put(maps, (4, NZ), eye)
    put(maps, (4, NZ - 1), gin[NZ - 1])
    for n in range(NZ - 1):
        tile_of(n, NZ - 1)
    for n in range(NZ):
        prods[1, n] = product(n, NZ - 1)
        prods[0, n + 1] = product(0, n)
        put(maps, (2, n + 1), product(0, n))
    pin[x] = product(0, NZ - 1)

    def p_copy(d):
        return remote(pin.at[x], pin.at[x], p_s.at[d], p_r.at[d], to_x(d))

    each(NX, lambda d: p_copy(d).start(), 1)

    def segments_arrive():
        each(NX, lambda d: p_copy(d).wait_recv(), 1)
        for xs in range(1, NX - 1):
            put(segs, (0, xs), pin[xs])

    def turn_kernels(layer):
        def turn(t):
            block = w[layer, pl.ds(pl.multiple_of((8 - t) * CH, CH), CH), :].astype(F32)
            wt[layer, pl.ds(pl.multiple_of(t * CH, CH), CH), :] = block.T.astype(BF16)
        each(9, turn)

    def first_slot():
        segments_arrive()
        turn_kernels(1)

    for b in range(BANDS):
        scan(0, b, False, (first_slot, lambda: turn_kernels(0), None)[b])

    for b in range(BANDS):
        arrive(0, b)
        for p, q in split(EDGES[0][b], EDGES[0][b + 1]):
            e = ein[0, px(p, q), :]
            ends[px(p, q), :] = prop[px(p, q), :] + times(e, maps[0, z])
            value = start[px(p, q), :] + e
            start[px(p, q), :] = value
            fill(x3a, p, q, jnp.tanh(value))
        relax(1, b, 1, ends)

    def turn_maps(s):
        put(maps, (3, s + 1), prods[0, s + 1].T)

    def second_slot():
        put(maps, (3, 0), eye)
        each(NZ - 1, turn_maps)

    def third_slot():
        loads[3].wait()
        for p, q in split(0, SIDE):
            fill(z3a, p, q, cot[px(p, q), :])
        for p, q in split(0, SIDE):
            ycot[px(p, q), :] = conv(z3a, p, q, wt[1])

    for b in range(BANDS):
        scan(1, b, False, (second_slot, third_slot, None)[b])

    def pull(k, b, old):
        first, last = EDGES[k][b], EDGES[k][b + 1]
        for p, q in split(first, last):
            value = mid[px(p, q), :] + d0[px(p, q), :] * conv(z3b, p, q, wt[0])
            prop[px(p, q), :] = value
            resout[k, px(p, q), :] = value - old[px(p, q), :]
        send_residual(k, b)

    def behind(k, b):
        lo = 0 if b == 0 else EDGES[k][b] + 1
        hi = SIDE if b == BANDS - 1 else EDGES[k][b + 1] + 1
        return split(lo, hi)

    for b in range(BANDS):
        arrive(1, b)
        for p, q in split(EDGES[1][b], EDGES[1][b + 1]):
            e = ein[1, px(p, q), :]
            ends[px(p, q), :] = prop[px(p, q), :] + times(e, maps[0, z])
            value = start[px(p, q), :] + e
            start[px(p, q), :] = value
            active = jnp.tanh(value)
            d0[px(p, q), :] = STEP * (1.0 - active * active)
            fill(x3a, p, q, active)
        for p, q in behind(2, b):
            active = jnp.tanh(start[px(p, q), :] + STEP * conv(x3a, p, q, w[0]))
            slope = STEP * (1.0 - active * active)
            d1[px(p, q), :] = slope
            fill(x3b, p, q, active)
            value = cot[px(p, q), :] + slope * ycot[px(p, q), :]
            mid[px(p, q), :] = value
            fill(z3b, p, q, value)
        pull(2, b, cot)

    def turn_steps(s):
        put(maps, (1, s), gin[s].T)

    def turn_carries(s):
        put(maps, (5, s), prods[1, s].T)

    def fourth_slot():
        each(NZ, turn_carries)
        each(NZ, lambda d: g_copy(d).wait_send(), 1)
        each(NZ, lambda d: g_forward(d).wait_send(), 1)
        each(NX, lambda d: p_copy(d).wait_send(), 1)
        for xs in range(1, NX - 1):
            put(segs, (1, xs), pin[xs].T)

    each(NZ, turn_steps)
    for b in range(BANDS):
        scan(2, b, True, (fourth_slot, None, None)[b])

    for b in range(BANDS):
        arrive(2, b)
        for p, q in split(EDGES[2][b], EDGES[2][b + 1]):
            f = ein[2, px(p, q), :]
            adj[px(p, q), :] = prop[px(p, q), :] + times(f, maps[1, z])
            value = cot[px(p, q), :] + f
            start[px(p, q), :] = value
            fill(z3a, p, q, value)
        for p, q in behind(3, b):
            value = start[px(p, q), :] + d1[px(p, q), :] * conv(z3a, p, q, wt[1])
            mid[px(p, q), :] = value
            fill(z3b, p, q, value)
        pull(3, b, adj)

    for b in range(BANDS):
        scan(3, b, True)

    def place(core, yy):
        return pl.ds(pl.multiple_of(core * half + yy * part, part), part)

    other = pl.ds(pl.multiple_of((NC - 1 - c) * half, half), half)

    def sib_copy(layer):
        return remote(local_grad.at[layer, other], gs.at[layer], sib_s.at[layer], sib_r.at[layer], to_core())

    def rs_copy(layer, d):
        return remote(hsum.at[layer, lax.rem(y + d, NY)], yin.at[layer, d], rs_s.at[layer, d], rs_r.at[layer, d], to_y(d))

    def ag_copy(layer, d):
        at = place(c, y)
        return remote(grad.at[layer, at], grad.at[layer, at], ag_s.at[layer, d], ag_r.at[layer, d], to_y(d))

    def fw_copy(layer, d):
        at = place(c, lax.rem(y + NY - d, NY))
        return remote(grad.at[layer, at], grad.at[layer, at], fw_s.at[layer, d], fw_r.at[layer, d], to_core())

    def reduce_core(layer):
        sib_copy(layer).wait()
        for yy in range(NY):
            hsum[layer, yy] = local_grad[layer, place(c, yy), :] + gs[layer, pl.ds(yy * part, part), :]
        each(NY, lambda d: rs_copy(layer, d).start(), 1)

    def reduce_chips(layer):
        total = hsum[layer, y]
        for d in range(1, NY):
            rs_copy(layer, d).wait_recv()
            total = total + yin[layer, d]
        grad[layer, place(c, y), :] = total * factor
        each(NY, lambda d: ag_copy(layer, d).start(), 1)
        fw_copy(layer, 0).start()

    def spread(layer):
        def go(d):
            ag_copy(layer, d).wait_recv()
            fw_copy(layer, d).start()
        each(NY, go, 1)

    def gradient(layer, signal, buffer, first, last, more):
        for r in range(3):
            block = jnp.dot(signal[:, px(first, last)], buffer[px(first + r, last + r), :], preferred_element_type=F32)
            for s in range(3):
                t = 3 * r + s
                value = block[:, CH * s : CH * (s + 1)].T
                at = slice(CH * t, CH * (t + 1))
                local_grad[layer, at, :] = local_grad[layer, at, :] + value if more else value

    def adjoint_out(b):
        for p, q in split(EDGES[3][b], EDGES[3][b + 1]):
            adj[px(p, q), :] = prop[px(p, q), :] + times(ein[3, px(p, q), :], maps[1, z])

    def top_signal(p, q):
        value = start[px(p, q), :] + ein[3, px(p, q), :]
        start[px(p, q), :] = value
        fill(z3a, p, q, value)
        zt[:, px(p, q)] = value.T.astype(BF16)

    def lower_signal(p, q):
        value = start[px(p, q), :] + d1[px(p, q), :] * conv(z3a, p, q, wt[1])
        zt0[:, px(p, q)] = value.T.astype(BF16)

    cuts = [e // 4 * 4 for e in EDGES[3]]
    lows = [0] + [(e - 1) // 4 * 4 for e in cuts[1:-1]] + [SIDE]

    def halves(first, last):
        middle = (first + last) // 8 * 4
        return [(p, q) for p, q in ((first, middle), (middle, last)) if q > p]

    for b in range(BANDS):
        arrive(3, b)
        for p, q in halves(cuts[b], cuts[b + 1]):
            top_signal(p, q)
        gradient(1, zt, x3b, cuts[b], cuts[b + 1], b > 0)
        if b == BANDS - 1:
            sib_copy(1).start()
        for p, q in halves(lows[b], lows[b + 1]):
            lower_signal(p, q)
        if b == BANDS - 1:
            reduce_core(1)
        gradient(0, zt0, x3a, lows[b], lows[b + 1], b > 0)
        if b < BANDS - 1:
            adjoint_out(b)
    sib_copy(0).start()
    adjoint_out(BANDS - 1)
    reduce_core(0)
    reduce_chips(1)
    reduce_chips(0)
    for b in range(BANDS):
        sent(3, b)
    spread(1)
    spread(0)
    for layer in range(2):
        each(NY, lambda d: fw_copy(layer, d).wait_recv(), 0)

    for layer in range(2):
        each(NY, lambda d: rs_copy(layer, d).wait_send(), 1)
        each(NY, lambda d: ag_copy(layer, d).wait_send(), 1)
        each(NY, lambda d: fw_copy(layer, d).wait_send(), 0)


def make_local(NX, NZ, NY, NC):
    half = TAPS // NC
    part = half // NY
    dma = pltpu.SemaphoreType.DMA
    vmem = pltpu.VMEM
    image = vmem((PIXELS, CH), F32)
    padded = vmem((PIXELS + 2 * SIDE, 3 * CH), BF16)
    sweeps = vmem((4, PIXELS, CH), F32)
    moves = dma((4 * BANDS, NZ))

    def local(features, cotangent, weights, coarse_map):
        factor = STEP / (features.shape[0] * NY * NC)
        out = pl.pallas_call(
            functools.partial(body, NX, NZ, NY, NC, factor),
            out_shape=(
                jax.ShapeDtypeStruct((PIXELS, CH), F32),
                jax.ShapeDtypeStruct((PIXELS, CH), F32),
                jax.ShapeDtypeStruct((2, TAPS, CH), F32),
            ),
            in_specs=[pl.BlockSpec(memory_space=pltpu.HBM)] * 4,
            out_specs=[pl.BlockSpec(memory_space=vmem)] * 3,
            scratch_shapes=[
                image, image, vmem((2, TAPS, CH), BF16), vmem((CH, CH), F32),
                padded, padded, padded, padded,
                vmem((2, TAPS, CH), BF16),
                image, image, image, image, image, image,
                vmem((CH, PIXELS), BF16), vmem((CH, PIXELS), BF16),
                sweeps, sweeps, sweeps, sweeps,
                vmem((4, NX, PIXELS // NZ, CH), F32),
                vmem((NZ, CH, CH), F32),
                vmem((NX, CH, CH), F32),
                vmem((2, NZ + 1, CH, CH), F32),
                vmem((NZ, 2 * CH, 2 * CH), BF16),
                vmem((6, NZ + 1, 2 * CH, 2 * CH), BF16),
                vmem((2, NX, 2 * CH, 2 * CH), BF16),
                vmem((2, TAPS, CH), F32),
                vmem((2, half, CH), F32),
                vmem((2, NY, part, CH), F32),
                vmem((2, NY, part, CH), F32),
                dma((4,)),
                moves, moves, moves, moves, dma((4 * BANDS, NX)), dma((4 * BANDS, NX)),
                dma((NZ,)), dma((NZ,)), dma((NZ,)), dma((NZ,)), dma((NX,)), dma((NX,)),
                dma((2,)), dma((2,)), dma((2, NY)), dma((2, NY)), dma((2, NY)), dma((2, NY)), dma((2, NY)), dma((2, NY)),
            ],
            compiler_params=pltpu.CompilerParams(
                collective_id=0, has_side_effects=True, vmem_limit_bytes=56 * 1024 * 1024
            ),
            cost_estimate=pl.CostEstimate(flops=5 * 10**9, bytes_accessed=5 * 10**6, transcendentals=10**6),
        )(
            features.reshape(PIXELS, CH),
            cotangent.reshape(PIXELS, CH),
            weights.reshape(2, TAPS, CH),
            coarse_map.reshape(CH, CH),
        )
        shape = (1, 1, SIDE, SIDE, CH)
        return out[0].reshape(shape), out[1].reshape(shape), out[2].reshape(2, 9, CH, CH)

    return local


def build(mesh, sizes):
    return jax.shard_map(
        make_local(*sizes),
        mesh=mesh,
        in_specs=(P("dp", None, None, None), P("dp", None, None, None), P("tm", None, None, None), P("tm", None, None)),
        out_specs=(P("tm", "dp", None, None, None), P("tm", "dp", None, None, None), P("tm", None, None, None)),
        check_vma=False,
    )


def solution(mesh):
    return build(mesh, (4, 8, 4, 2))
```

```python
import functools

import jax
import jax.numpy as jnp
from jax import lax
from jax.experimental import pallas as pl
from jax.experimental.pallas import tpu as pltpu
from jax.sharding import PartitionSpec as P

MESH = pl.DeviceIdType.MESH
STEP = 0.25
DIAGONAL = 0.9
SIDE = 32
PIXELS = SIDE * SIDE
CH = 128
BANDS = 2
EDGES = ((0, 20, 32), (0, 18, 32), (0, 16, 32), (0, 14, 32))
TAPS = 9 * CH
F32, BF16 = jnp.float32, jnp.bfloat16


def two_terms(value):
    high = value.astype(BF16)
    return high, (value - high.astype(F32)).astype(BF16)


def times(value, tile):
    high, low = two_terms(value)
    both = jnp.dot(jnp.concatenate([high, low], 1), tile, preferred_element_type=F32)
    return both[:, :CH] + both[:, CH:]


def split(first, last, most=12):
    count = -(-(last - first) // most)
    cuts = [first + (last - first) * n // (2 * count) * 2 for n in range(count)] + [last]
    return list(zip(cuts[:-1], cuts[1:]))


def body(
    NX, NZ, NY, NC, factor,
    feat_in, cot_in, w_in, cm_in,
    ends, adj, grad,
    feat, cot, w, cm,
    x3a, x3b, z3a, z3b, wt, ww, wwt, start, mid, prop, d0, d1, ycot, zt, zt0,
    resout, resin, eout, ein, tin, gin, pin, prods, temps, maps, segs, local_grad, gs, hsum, yin,
    in_s,
    res_s, res_r, e_s, e_r, t_s, t_r, g_s, g_r, gf_s, gf_r, p_s, p_r, sib_s, sib_r, rs_s, rs_r, ag_s, ag_r, fw_s, fw_r,
):
    loads = [
        pltpu.make_async_copy(src, dst, in_s.at[n])
        for n, (src, dst) in enumerate(((cm_in, cm), (feat_in, feat), (w_in, w), (cot_in, cot)))
    ]
    for load in loads:
        load.start()

    tm, dp = lax.axis_index("tm"), lax.axis_index("dp")
    x, z = tm // NZ, lax.rem(tm, NZ)
    y, c = dp // NC, lax.rem(dp, NC)
    half = TAPS // NC
    part = half // NY
    far_first = sorted(range(1, NZ), key=lambda d: -min(d, NZ - d))

    def to_z(d):
        return {"tm": x * NZ + lax.rem(z + d, NZ)}

    def to_x(d):
        return {"tm": lax.rem(x + d, NX) * NZ + z}

    def to_y(d):
        return {"dp": lax.rem(y + d, NY) * NC + c}

    def to_core():
        return {"dp": y * NC + (NC - 1 - c)}

    def remote(src, dst, send, recv, device):
        return pltpu.make_async_remote_copy(
            src_ref=src, dst_ref=dst, send_sem=send, recv_sem=recv, device_id=device, device_id_type=MESH
        )

    def each(count, f, first=0):
        def go(i, carry):
            f(i)
            return carry
        lax.fori_loop(first, count, go, 0)

    barrier = pltpu.get_barrier_semaphore()

    def greet(device):
        pl.semaphore_signal(barrier, inc=1, device_id=device, device_id_type=MESH)

    each(NZ, lambda d: greet(to_z(d)), 1)
    each(NX, lambda d: greet(to_x(d)), 1)
    each(NY, lambda d: greet(to_y(d)), 1)
    greet(to_core())

    def px(first, last):
        return slice(first * SIDE, last * SIDE)

    def fill(buffer, first, last, value):
        size = (last - first) * SIDE
        column = lax.rem(lax.broadcasted_iota(jnp.int32, (size, CH), 0), SIDE)
        left = jnp.where(column == 0, 0.0, pltpu.roll(value, 1, 0))
        right = jnp.where(column == SIDE - 1, 0.0, pltpu.roll(value, size - 1, 0))
        at = px(first + 1, last + 1)
        buffer[at, :CH] = left.astype(BF16)
        buffer[at, CH : 2 * CH] = value.astype(BF16)
        buffer[at, 2 * CH :] = right.astype(BF16)

    def conv(buffer, first, last, kernel):
        odd = (last - first) % 2
        top = first - odd if last == SIDE else first
        pairs = range((last - first + odd) // 2)
        pieces = [
            jnp.concatenate([buffer[px(top + 2 * m + r, top + 2 * m + r + 1), :] for m in pairs], 0) for r in range(4)
        ]
        both = jnp.dot(jnp.concatenate(pieces, 1), kernel[...], preferred_element_type=F32)
        rows = [both[px(m, m + 1), CH * h : CH * (h + 1)] for m in pairs for h in range(2)]
        return jnp.concatenate(rows[first - top : last - top], 0)

    def widen(wide, layer, source):
        for r in range(4):
            at = slice(3 * CH * r, 3 * CH * (r + 1))
            zero = jnp.zeros((3 * CH, CH), BF16)
            wide[layer, at, :CH] = source[layer, 3 * CH * r : 3 * CH * (r + 1), :] if r < 3 else zero
            wide[layer, at, CH:] = source[layer, 3 * CH * (r - 1) : 3 * CH * r, :] if r > 0 else zero

    zero_row = jnp.zeros((SIDE, 3 * CH), BF16)
    for buffer in (x3a, x3b, z3a, z3b):
        buffer[:SIDE, :] = zero_row
        buffer[PIXELS + SIDE :, :] = zero_row
    eye = (lax.broadcasted_iota(jnp.int32, (CH, CH), 0) == lax.broadcasted_iota(jnp.int32, (CH, CH), 1)).astype(F32)
    loads[0].wait()
    gin[z] = DIAGONAL * eye + cm[...]

    loads[1].wait()
    for p, q in split(0, SIDE):
        value = feat[px(p, q), :]
        start[px(p, q), :] = value
        fill(x3a, p, q, jnp.tanh(value))
    loads[2].wait()
    widen(ww, 0, w)
    widen(ww, 1, w)
    pl.semaphore_wait(barrier, NZ - 1 + NX - 1 + NY - 1 + 1)

    gh = pl.ds(pl.multiple_of(c * (CH // NC), CH // NC), CH // NC)

    def g_copy(d):
        return remote(gin.at[z, gh], gin.at[z, gh], g_s.at[d], g_r.at[d], to_z(d))

    def g_forward(d):
        zs = lax.rem(z + NZ - d, NZ)
        return remote(gin.at[zs, gh], gin.at[zs, gh], gf_s.at[d], gf_r.at[d], to_core())

    for d in far_first:
        g_copy(d).start()

    def share(k, b):
        first, last = EDGES[k][b], EDGES[k][b + 1]
        return first * SIDE, (last - first) * SIDE // NZ

    def spot(k, b, n):
        base, R = share(k, b)
        if isinstance(n, int):
            return slice(base + n * R, base + n * R + R)
        return pl.ds(pl.multiple_of(base + n * R, 8), R)

    def res_copy(k, b, d):
        zp = lax.rem(z + d, NZ)
        m = BANDS * k + b
        return remote(
            resout.at[k, spot(k, b, zp)], resin.at[k, spot(k, b, z)], res_s.at[m, d], res_r.at[m, d], to_z(d)
        )

    def send_residual(k, b):
        for d in far_first:
            res_copy(k, b, d).start()
        resin[k, spot(k, b, z), :] = resout[k, spot(k, b, z), :]

    def t_spot(k, b):
        base, R = share(k, b)
        return slice(base // NZ, base // NZ + R)

    def t_copy(k, b, d):
        m = BANDS * k + b
        at = t_spot(k, b)
        return remote(tin.at[k, x, at], tin.at[k, x, at], t_s.at[m, d], t_r.at[m, d], to_x(d))

    def e_copy(k, b, d):
        zp = lax.rem(z + d, NZ)
        m = BANDS * k + b
        return remote(eout.at[k, spot(k, b, zp)], ein.at[k, spot(k, b, z)], e_s.at[m, d], e_r.at[m, d], to_z(d))

    def put(where, index, matrix):
        high, low = two_terms(matrix)
        where[(*index, slice(0, CH), slice(0, CH))] = high
        where[(*index, slice(0, CH), slice(CH, None))] = low
        where[(*index, slice(CH, None), slice(0, CH))] = high
        where[(*index, slice(CH, None), slice(CH, None))] = jnp.zeros((CH, CH), BF16)

    def sent(k, b):
        for d in far_first:
            res_copy(k, b, d).wait_send()
            e_copy(k, b, d).wait_send()
        for d in range(1, NX):
            t_copy(k, b, d).wait_send()

    def scan(k, b, backward, meanwhile=None):
        total_kind, chain_kind, carry_kind = (3, 1, 5) if backward else (4, 0, 2)
        at = t_spot(k, b)
        edge = NZ - 1 if backward else 0

        def term(d):
            s = lax.rem(z + NZ - d, NZ)
            return times(resin[k, spot(k, b, s), :], maps[total_kind, s + (0 if backward else 1)])

        near = far_first[::-1][: NZ // 2]
        for d in near:
            res_copy(k, b, d).wait_recv()
        total = term(0)
        for d in near:
            total = total + term(d)
        for d in far_first[::-1][NZ // 2 :]:
            res_copy(k, b, d).wait_recv()
        for d in far_first[::-1][NZ // 2 :]:
            total = total + term(d)
        tin[k, x, at, :] = total
        for d in range(1, NX):
            t_copy(k, b, d).start()
        run = {}
        if backward:
            value = resin[k, spot(k, b, NZ - 1), :]
            run[NZ - 2] = value
            for s in range(NZ - 2, 0, -1):
                value = times(value, maps[chain_kind, s]) + resin[k, spot(k, b, s), :]
                run[s - 1] = value
        else:
            value = resin[k, spot(k, b, 0), :]
            run[1] = value
            for s in range(1, NZ - 1):
                value = times(value, maps[chain_kind, s]) + resin[k, spot(k, b, s), :]
                run[s + 1] = value
        for n in run:
            eout[k, spot(k, b, n), :] = run[n]
        if meanwhile is not None:
            meanwhile()
        if k > 0:
            sent(k - 1, b)
        for d in range(1, NX):
            t_copy(k, b, d).wait_recv()
        carry = jnp.zeros((total.shape[0], CH), F32)
        for lag in range(1, NX):
            xs = lax.rem(x + (lag if backward else NX - lag), NX)
            value = tin[k, xs, at, :]
            if lag > 1:
                value = times(value, segs[1 if backward else 0, lag])
            carry = carry + jnp.where(x < NX - lag if backward else x >= lag, value, 0.0)
        for n in range(NZ):
            if n == edge:
                eout[k, spot(k, b, n), :] = carry
            else:
                tile = maps[carry_kind, n + (1 if backward else 0)]
                eout[k, spot(k, b, n), :] = eout[k, spot(k, b, n), :] + times(carry, tile)
        for d in far_first:
            e_copy(k, b, d).start()
        ein[k, spot(k, b, z), :] = eout[k, spot(k, b, z), :]

    def arrive(k, b):
        for d in far_first[::-1]:
            e_copy(k, b, d).wait_recv()

    def relax(k, b, ahead, old):
        first, last = EDGES[k][b], EDGES[k][b + 1]
        lo = 0 if b == 0 else first + ahead
        hi = SIDE if b == BANDS - 1 else last + ahead
        for p, q in split(lo, hi):
            value = start[px(p, q), :] + STEP * conv(x3a, p, q, ww.at[0])
            mid[px(p, q), :] = value
            fill(x3b, p, q, jnp.tanh(value))
        for p, q in split(first, last):
            value = mid[px(p, q), :] + STEP * conv(x3b, p, q, ww.at[1])
            prop[px(p, q), :] = value
            resout[k, px(p, q), :] = value - old[px(p, q), :]
        send_residual(k, b)


    relax(0, 0, 1, feat)

    def g_pass(d):
        g_copy(d).wait_recv()
        g_forward(d).start()

    each(NZ, g_pass, 1)
    for b in range(1, BANDS):
        relax(0, b, 1, feat)

    each(NZ, lambda d: g_forward(d).wait_recv(), 1)
    made, tiles = {}, {}

    def product(i, j):
        if (i, j) not in made:
            if i == j:
                value = gin[i]
            else:
                step = 1
                while (j // (2 * step)) * 2 * step > i:
                    step *= 2
                m = j // step * step
                value = times(product(i, m - 1), tile_of(m, j))
            made[i, j] = value
        return made[i, j]

    def tile_of(i, j):
        if (i, j) not in tiles:
            value = product(i, j)
            if i == j:
                put(maps, (0, i), value)
                tiles[i, j] = maps.at[0, i]
            elif j == NZ - 1:
                put(maps, (4, i), value)
                tiles[i, j] = maps.at[4, i]
            else:
                n = sum(i2 != j2 and j2 != NZ - 1 for i2, j2 in tiles)
                put(temps, (n,), value)
                tiles[i, j] = temps.at[n]
        return tiles[i, j][...]

    for n in range(NZ):
        tile_of(n, n)
    put(maps, (4, NZ), eye)
    put(maps, (4, NZ - 1), gin[NZ - 1])
    for n in range(NZ - 1):
        tile_of(n, NZ - 1)
    for n in range(NZ):
        prods[1, n] = product(n, NZ - 1)
        prods[0, n + 1] = product(0, n)
        put(maps, (2, n + 1), product(0, n))
    pin[x] = product(0, NZ - 1)

    def p_copy(d):
        return remote(pin.at[x], pin.at[x], p_s.at[d], p_r.at[d], to_x(d))

    each(NX, lambda d: p_copy(d).start(), 1)

    def segments_arrive():
        each(NX, lambda d: p_copy(d).wait_recv(), 1)
        if NX > 2:
            def segment(lag):
                return pin[lax.rem(x + NX + lag, NX)]

            back, ahead = segment(-1), segment(1)
            put(segs, (0, 2), back)
            prods[2, 2] = ahead
            for lag in range(3, NX):
                back = times(segment(1 - lag), segs[0, lag - 1])
                put(segs, (0, lag), back)
                put(segs, (1, lag), segment(lag - 1))
                ahead = times(ahead, segs[1, lag])
                prods[2, lag] = ahead

    def turn_kernels(layer):
        def turn(t):
            block = w[layer, pl.ds(pl.multiple_of((8 - t) * CH, CH), CH), :].astype(F32)
            wt[layer, pl.ds(pl.multiple_of(t * CH, CH), CH), :] = block.T.astype(BF16)
        each(9, turn)
        widen(wwt, layer, wt)

    def first_slot():
        segments_arrive()
        turn_kernels(1)

    for b in range(BANDS):
        scan(0, b, False, (first_slot, lambda: turn_kernels(0), None)[b])

    for b in range(BANDS):
        arrive(0, b)
        for p, q in split(EDGES[0][b], EDGES[0][b + 1]):
            e = ein[0, px(p, q), :]
            ends[px(p, q), :] = prop[px(p, q), :] + times(e, maps[0, z])
            value = start[px(p, q), :] + e
            start[px(p, q), :] = value
            fill(x3a, p, q, jnp.tanh(value))
        relax(1, b, 1, ends)

    def turn_maps(s):
        put(maps, (3, s + 1), prods[0, s + 1].T)

    def second_slot():
        put(maps, (3, 0), eye)
        each(NZ - 1, turn_maps)

    def third_slot():
        loads[3].wait()
        for p, q in split(0, SIDE):
            fill(z3a, p, q, cot[px(p, q), :])
        for p, q in split(0, SIDE):
            ycot[px(p, q), :] = conv(z3a, p, q, wwt.at[1])

    for b in range(BANDS):
        scan(1, b, False, (second_slot, third_slot, None)[b])

    def pull(k, b, old):
        first, last = EDGES[k][b], EDGES[k][b + 1]
        for p, q in split(first, last):
            value = mid[px(p, q), :] + d0[px(p, q), :] * conv(z3b, p, q, wwt.at[0])
            prop[px(p, q), :] = value
            resout[k, px(p, q), :] = value - old[px(p, q), :]
        send_residual(k, b)

    def behind(k, b):
        lo = 0 if b == 0 else EDGES[k][b] + 1
        hi = SIDE if b == BANDS - 1 else EDGES[k][b + 1] + 1
        return split(lo, hi)

    for b in range(BANDS):
        arrive(1, b)
        for p, q in split(EDGES[1][b], EDGES[1][b + 1]):
            e = ein[1, px(p, q), :]
            ends[px(p, q), :] = prop[px(p, q), :] + times(e, maps[0, z])
            value = start[px(p, q), :] + e
            start[px(p, q), :] = value
            active = jnp.tanh(value)
            d0[px(p, q), :] = STEP * (1.0 - active * active)
            fill(x3a, p, q, active)
        for p, q in behind(2, b):
            active = jnp.tanh(start[px(p, q), :] + STEP * conv(x3a, p, q, ww.at[0]))
            slope = STEP * (1.0 - active * active)
            d1[px(p, q), :] = slope
            fill(x3b, p, q, active)
            value = cot[px(p, q), :] + slope * ycot[px(p, q), :]
            mid[px(p, q), :] = value
            fill(z3b, p, q, value)
        pull(2, b, cot)

    def turn_steps(s):
        put(maps, (1, s), gin[s].T)

    def turn_carries(s):
        put(maps, (5, s), prods[1, s].T)

    def fourth_slot():
        each(NZ, turn_carries)
        each(NZ, lambda d: g_copy(d).wait_send(), 1)
        each(NZ, lambda d: g_forward(d).wait_send(), 1)
        each(NX, lambda d: p_copy(d).wait_send(), 1)
        for lag in range(2, NX):
            put(segs, (1, lag), prods[2, lag].T)

    each(NZ, turn_steps)
    for b in range(BANDS):
        scan(2, b, True, (fourth_slot, None, None)[b])

    for b in range(BANDS):
        arrive(2, b)
        for p, q in split(EDGES[2][b], EDGES[2][b + 1]):
            f = ein[2, px(p, q), :]
            adj[px(p, q), :] = prop[px(p, q), :] + times(f, maps[1, z])
            value = cot[px(p, q), :] + f
            start[px(p, q), :] = value
            fill(z3a, p, q, value)
        for p, q in behind(3, b):
            value = start[px(p, q), :] + d1[px(p, q), :] * conv(z3a, p, q, wwt.at[1])
            mid[px(p, q), :] = value
            fill(z3b, p, q, value)
        pull(3, b, adj)

    for b in range(BANDS):
        scan(3, b, True)

    def place(core, yy):
        return pl.ds(pl.multiple_of(core * half + yy * part, part), part)

    other = pl.ds(pl.multiple_of((NC - 1 - c) * half, half), half)

    def sib_copy(layer):
        return remote(local_grad.at[layer, other], gs.at[layer], sib_s.at[layer], sib_r.at[layer], to_core())

    def rs_copy(layer, d):
        return remote(hsum.at[layer, lax.rem(y + d, NY)], yin.at[layer, d], rs_s.at[layer, d], rs_r.at[layer, d], to_y(d))

    def ag_copy(layer, d):
        at = place(c, y)
        return remote(grad.at[layer, at], grad.at[layer, at], ag_s.at[layer, d], ag_r.at[layer, d], to_y(d))

    def fw_copy(layer, d):
        at = place(c, lax.rem(y + NY - d, NY))
        return remote(grad.at[layer, at], grad.at[layer, at], fw_s.at[layer, d], fw_r.at[layer, d], to_core())

    def reduce_core(layer):
        sib_copy(layer).wait()
        for yy in range(NY):
            hsum[layer, yy] = local_grad[layer, place(c, yy), :] + gs[layer, pl.ds(yy * part, part), :]
        each(NY, lambda d: rs_copy(layer, d).start(), 1)

    def reduce_chips(layer):
        total = hsum[layer, y]
        for d in range(1, NY):
            rs_copy(layer, d).wait_recv()
            total = total + yin[layer, d]
        grad[layer, place(c, y), :] = total * factor
        each(NY, lambda d: ag_copy(layer, d).start(), 1)
        fw_copy(layer, 0).start()

    def spread(layer):
        def go(d):
            ag_copy(layer, d).wait_recv()
            fw_copy(layer, d).start()
        each(NY, go, 1)

    def gradient(layer, signal, buffer, first, last, more):
        for r in range(3):
            block = jnp.dot(signal[:, px(first, last)], buffer[px(first + r, last + r), :], preferred_element_type=F32)
            for s in range(3):
                t = 3 * r + s
                value = block[:, CH * s : CH * (s + 1)].T
                at = slice(CH * t, CH * (t + 1))
                local_grad[layer, at, :] = local_grad[layer, at, :] + value if more else value

    def adjoint_out(b):
        for p, q in split(EDGES[3][b], EDGES[3][b + 1]):
            adj[px(p, q), :] = prop[px(p, q), :] + times(ein[3, px(p, q), :], maps[1, z])

    def top_signal(p, q):
        value = start[px(p, q), :] + ein[3, px(p, q), :]
        start[px(p, q), :] = value
        fill(z3a, p, q, value)
        zt[:, px(p, q)] = value.T.astype(BF16)

    def lower_signal(p, q):
        value = start[px(p, q), :] + d1[px(p, q), :] * conv(z3a, p, q, wwt.at[1])
        zt0[:, px(p, q)] = value.T.astype(BF16)

    cuts = [e // 4 * 4 for e in EDGES[3]]
    lows = [0] + [(e - 1) // 4 * 4 for e in cuts[1:-1]] + [SIDE]

    def halves(first, last):
        middle = (first + last) // 8 * 4
        return [(p, q) for p, q in ((first, middle), (middle, last)) if q > p]

    for b in range(BANDS):
        arrive(3, b)
        for p, q in halves(cuts[b], cuts[b + 1]):
            top_signal(p, q)
        gradient(1, zt, x3b, cuts[b], cuts[b + 1], b > 0)
        if b == BANDS - 1:
            sib_copy(1).start()
        for p, q in halves(lows[b], lows[b + 1]):
            lower_signal(p, q)
        if b == BANDS - 1:
            reduce_core(1)
        gradient(0, zt0, x3a, lows[b], lows[b + 1], b > 0)
        if b < BANDS - 1:
            adjoint_out(b)
    sib_copy(0).start()
    adjoint_out(BANDS - 1)
    reduce_core(0)
    reduce_chips(1)
    reduce_chips(0)
    for b in range(BANDS):
        sent(3, b)
    spread(1)
    spread(0)
    for layer in range(2):
        each(NY, lambda d: fw_copy(layer, d).wait_recv(), 0)

    for layer in range(2):
        each(NY, lambda d: rs_copy(layer, d).wait_send(), 1)
        each(NY, lambda d: ag_copy(layer, d).wait_send(), 1)
        each(NY, lambda d: fw_copy(layer, d).wait_send(), 0)


def make_local(NX, NZ, NY, NC):
    half = TAPS // NC
    part = half // NY
    dma = pltpu.SemaphoreType.DMA
    vmem = pltpu.VMEM
    image = vmem((PIXELS, CH), F32)
    padded = vmem((PIXELS + 2 * SIDE, 3 * CH), BF16)
    sweeps = vmem((4, PIXELS, CH), F32)
    moves = dma((4 * BANDS, NZ))

    def local(features, cotangent, weights, coarse_map):
        factor = STEP / (features.shape[0] * NY * NC)
        out = pl.pallas_call(
            functools.partial(body, NX, NZ, NY, NC, factor),
            out_shape=(
                jax.ShapeDtypeStruct((PIXELS, CH), F32),
                jax.ShapeDtypeStruct((PIXELS, CH), F32),
                jax.ShapeDtypeStruct((2, TAPS, CH), F32),
            ),
            in_specs=[pl.BlockSpec(memory_space=pltpu.HBM)] * 4,
            out_specs=[pl.BlockSpec(memory_space=vmem)] * 3,
            scratch_shapes=[
                image, image, vmem((2, TAPS, CH), BF16), vmem((CH, CH), F32),
                padded, padded, padded, padded,
                vmem((2, TAPS, CH), BF16),
                vmem((2, 12 * CH, 2 * CH), BF16), vmem((2, 12 * CH, 2 * CH), BF16),
                image, image, image, image, image, image,
                vmem((CH, PIXELS), BF16), vmem((CH, PIXELS), BF16),
                sweeps, sweeps, sweeps, sweeps,
                vmem((4, NX, PIXELS // NZ, CH), F32),
                vmem((NZ, CH, CH), F32),
                vmem((NX, CH, CH), F32),
                vmem((3, max(NX, NZ + 1), CH, CH), F32),
                vmem((NZ, 2 * CH, 2 * CH), BF16),
                vmem((6, NZ + 1, 2 * CH, 2 * CH), BF16),
                vmem((2, NX, 2 * CH, 2 * CH), BF16),
                vmem((2, TAPS, CH), F32),
                vmem((2, half, CH), F32),
                vmem((2, NY, part, CH), F32),
                vmem((2, NY, part, CH), F32),
                dma((4,)),
                moves, moves, moves, moves, dma((4 * BANDS, NX)), dma((4 * BANDS, NX)),
                dma((NZ,)), dma((NZ,)), dma((NZ,)), dma((NZ,)), dma((NX,)), dma((NX,)),
                dma((2,)), dma((2,)), dma((2, NY)), dma((2, NY)), dma((2, NY)), dma((2, NY)), dma((2, NY)), dma((2, NY)),
            ],
            compiler_params=pltpu.CompilerParams(
                collective_id=0, has_side_effects=True, vmem_limit_bytes=56 * 1024 * 1024
            ),
            cost_estimate=pl.CostEstimate(flops=5 * 10**9, bytes_accessed=5 * 10**6, transcendentals=10**6),
        )(
            features.reshape(PIXELS, CH),
            cotangent.reshape(PIXELS, CH),
            weights.reshape(2, TAPS, CH),
            coarse_map.reshape(CH, CH),
        )
        shape = (1, 1, SIDE, SIDE, CH)
        return out[0].reshape(shape), out[1].reshape(shape), out[2].reshape(2, 9, CH, CH)

    return local


def build(mesh, sizes):
    return jax.shard_map(
        make_local(*sizes),
        mesh=mesh,
        in_specs=(P("dp", None, None, None), P("dp", None, None, None), P("tm", None, None, None), P("tm", None, None)),
        out_specs=(P("tm", "dp", None, None, None), P("tm", "dp", None, None, None), P("tm", None, None, None)),
        check_vma=False,
    )


def solution(mesh):
    return build(mesh, (4, 8, 4, 2))
```

```python
import functools

import jax
import jax.numpy as jnp
from jax import lax
from jax.experimental import pallas as pl
from jax.experimental.pallas import tpu as pltpu
from jax.sharding import PartitionSpec as P

MESH = pl.DeviceIdType.MESH
STEP = 0.25
DIAGONAL = 0.9
SIDE = 32
PIXELS = SIDE * SIDE
CH = 128
BANDS = 2
EDGES = ((0, 20, 32), (0, 18, 32), (0, 16, 32), (0, 14, 32))
TAPS = 9 * CH
F32, BF16 = jnp.float32, jnp.bfloat16


def two_terms(value):
    high = value.astype(BF16)
    return high, (value - high.astype(F32)).astype(BF16)


def times(value, tile):
    high, low = two_terms(value)
    both = jnp.dot(jnp.concatenate([high, low], 1), tile, preferred_element_type=F32)
    return both[:, :CH] + both[:, CH:]


def split(first, last, most=12):
    count = -(-(last - first) // most)
    cuts = [first + (last - first) * n // (2 * count) * 2 for n in range(count)] + [last]
    return list(zip(cuts[:-1], cuts[1:]))


def body(
    NX, NZ, NY, NC, factor,
    feat_in, cot_in, w_in, cm_in,
    ends, adj, grad,
    feat, cot, w, cm,
    x3a, x3b, z3a, z3b, wt, ww, wwt, start, mid, prop, d0, d1, ycot, zt, zt0,
    resout, resin, eout, ein, tin, gin, pin, prods, temps, maps, segs, local_grad, gs, hsum, yin,
    in_s,
    res_s, res_r, e_s, e_r, t_s, t_r, g_s, g_r, gf_s, gf_r, p_s, p_r, sib_s, sib_r, rs_s, rs_r, ag_s, ag_r, fw_s, fw_r,
):
    loads = [
        pltpu.make_async_copy(src, dst, in_s.at[n])
        for n, (src, dst) in enumerate(((cm_in, cm), (feat_in, feat), (w_in, w), (cot_in, cot)))
    ]
    for load in loads:
        load.start()

    tm, dp = lax.axis_index("tm"), lax.axis_index("dp")
    x, z = tm // NZ, lax.rem(tm, NZ)
    y, c = dp // NC, lax.rem(dp, NC)
    half = TAPS // NC
    part = half // NY
    far_first = sorted(range(1, NZ), key=lambda d: -min(d, NZ - d))
    sooner, later = far_first[: NZ // 2], far_first[NZ // 2 :]

    def to_z(d):
        return {"tm": x * NZ + lax.rem(z + d, NZ)}

    def to_x(d):
        return {"tm": lax.rem(x + d, NX) * NZ + z}

    def to_y(d):
        return {"dp": lax.rem(y + d, NY) * NC + c}

    def to_core():
        return {"dp": y * NC + (NC - 1 - c)}

    def remote(src, dst, send, recv, device):
        return pltpu.make_async_remote_copy(
            src_ref=src, dst_ref=dst, send_sem=send, recv_sem=recv, device_id=device, device_id_type=MESH
        )

    def each(count, f, first=0):
        def go(i, carry):
            f(i)
            return carry
        lax.fori_loop(first, count, go, 0)

    barrier = pltpu.get_barrier_semaphore()

    def greet(device):
        pl.semaphore_signal(barrier, inc=1, device_id=device, device_id_type=MESH)

    each(NZ, lambda d: greet(to_z(d)), 1)
    each(NX, lambda d: greet(to_x(d)), 1)
    each(NY, lambda d: greet(to_y(d)), 1)
    greet(to_core())

    def px(first, last):
        return slice(first * SIDE, last * SIDE)

    def fill(buffer, first, last, value):
        size = (last - first) * SIDE
        column = lax.rem(lax.broadcasted_iota(jnp.int32, (size, CH), 0), SIDE)
        left = jnp.where(column == 0, 0.0, pltpu.roll(value, 1, 0))
        right = jnp.where(column == SIDE - 1, 0.0, pltpu.roll(value, size - 1, 0))
        at = px(first + 1, last + 1)
        buffer[at, :CH] = left.astype(BF16)
        buffer[at, CH : 2 * CH] = value.astype(BF16)
        buffer[at, 2 * CH :] = right.astype(BF16)

    def conv(buffer, first, last, kernel):
        odd = (last - first) % 2
        top = first - odd if last == SIDE else first
        pairs = range((last - first + odd) // 2)
        pieces = [
            jnp.concatenate([buffer[px(top + 2 * m + r, top + 2 * m + r + 1), :] for m in pairs], 0) for r in range(4)
        ]
        both = jnp.dot(jnp.concatenate(pieces, 1), kernel[...], preferred_element_type=F32)
        rows = [both[px(m, m + 1), CH * h : CH * (h + 1)] for m in pairs for h in range(2)]
        return jnp.concatenate(rows[first - top : last - top], 0)

    def widen(wide, layer, source):
        for r in range(4):
            at = slice(3 * CH * r, 3 * CH * (r + 1))
            zero = jnp.zeros((3 * CH, CH), BF16)
            wide[layer, at, :CH] = source[layer, 3 * CH * r : 3 * CH * (r + 1), :] if r < 3 else zero
            wide[layer, at, CH:] = source[layer, 3 * CH * (r - 1) : 3 * CH * r, :] if r > 0 else zero

    zero_row = jnp.zeros((SIDE, 3 * CH), BF16)
    for buffer in (x3a, x3b, z3a, z3b):
        buffer[:SIDE, :] = zero_row
        buffer[PIXELS + SIDE :, :] = zero_row
    eye = (lax.broadcasted_iota(jnp.int32, (CH, CH), 0) == lax.broadcasted_iota(jnp.int32, (CH, CH), 1)).astype(F32)
    loads[0].wait()
    gin[z] = DIAGONAL * eye + cm[...]

    loads[1].wait()
    for p, q in split(0, SIDE):
        value = feat[px(p, q), :]
        start[px(p, q), :] = value
        fill(x3a, p, q, jnp.tanh(value))
    loads[2].wait()
    widen(ww, 0, w)
    widen(ww, 1, w)
    pl.semaphore_wait(barrier, NZ - 1 + NX - 1 + NY - 1 + 1)

    gh = pl.ds(pl.multiple_of(c * (CH // NC), CH // NC), CH // NC)

    def g_copy(d):
        return remote(gin.at[z, gh], gin.at[z, gh], g_s.at[d], g_r.at[d], to_z(d))

    def g_forward(d):
        zs = lax.rem(z + NZ - d, NZ)
        return remote(gin.at[zs, gh], gin.at[zs, gh], gf_s.at[d], gf_r.at[d], to_core())

    for d in far_first:
        g_copy(d).start()

    def share(k, b):
        first, last = EDGES[k][b], EDGES[k][b + 1]
        return first * SIDE, (last - first) * SIDE // NZ

    def spot(k, b, n):
        base, R = share(k, b)
        if isinstance(n, int):
            return slice(base + n * R, base + n * R + R)
        return pl.ds(pl.multiple_of(base + n * R, 8), R)

    def res_copy(k, b, d):
        zp = lax.rem(z + d, NZ)
        m = BANDS * k + b
        return remote(
            resout.at[k, spot(k, b, zp)], resin.at[k, spot(k, b, z)], res_s.at[m, d], res_r.at[m, d], to_z(d)
        )

    def send_residual(k, b):
        for d in far_first if b == 0 else sooner:
            res_copy(k, b, d).start()
        resin[k, spot(k, b, z), :] = resout[k, spot(k, b, z), :]

    def t_spot(k, b):
        base, R = share(k, b)
        return slice(base // NZ, base // NZ + R)

    def t_copy(k, b, d):
        m = BANDS * k + b
        at = t_spot(k, b)
        return remote(tin.at[k, x, at], tin.at[k, x, at], t_s.at[m, d], t_r.at[m, d], to_x(d))

    def e_copy(k, b, d):
        zp = lax.rem(z + d, NZ)
        m = BANDS * k + b
        return remote(eout.at[k, spot(k, b, zp)], ein.at[k, spot(k, b, z)], e_s.at[m, d], e_r.at[m, d], to_z(d))

    def put(where, index, matrix):
        high, low = two_terms(matrix)
        where[(*index, slice(0, CH), slice(0, CH))] = high
        where[(*index, slice(0, CH), slice(CH, None))] = low
        where[(*index, slice(CH, None), slice(0, CH))] = high
        where[(*index, slice(CH, None), slice(CH, None))] = jnp.zeros((CH, CH), BF16)

    def sent(k, b):
        for d in far_first:
            res_copy(k, b, d).wait_send()
            e_copy(k, b, d).wait_send()
        for d in range(1, NX):
            t_copy(k, b, d).wait_send()

    def scan(k, b, backward, meanwhile=None):
        total_kind, chain_kind, carry_kind = (3, 1, 5) if backward else (4, 0, 2)
        at = t_spot(k, b)
        edge = NZ - 1 if backward else 0

        def term(d):
            s = lax.rem(z + NZ - d, NZ)
            return times(resin[k, spot(k, b, s), :], maps[total_kind, s + (0 if backward else 1)])

        near = far_first[::-1][: NZ // 2]
        for d in near:
            res_copy(k, b, d).wait_recv()
        total = term(0)
        for d in near:
            total = total + term(d)
        for d in far_first[::-1][NZ // 2 :]:
            res_copy(k, b, d).wait_recv()
        for d in far_first[::-1][NZ // 2 :]:
            total = total + term(d)
        tin[k, x, at, :] = total
        for d in range(1, NX):
            t_copy(k, b, d).start()
        for d in later:
            if b == 0:
                res_copy(k, 1, d).start()
            else:
                e_copy(k, 0, d).start()
        run = {}
        if backward:
            value = resin[k, spot(k, b, NZ - 1), :]
            run[NZ - 2] = value
            for s in range(NZ - 2, 0, -1):
                value = times(value, maps[chain_kind, s]) + resin[k, spot(k, b, s), :]
                run[s - 1] = value
        else:
            value = resin[k, spot(k, b, 0), :]
            run[1] = value
            for s in range(1, NZ - 1):
                value = times(value, maps[chain_kind, s]) + resin[k, spot(k, b, s), :]
                run[s + 1] = value
        for n in run:
            eout[k, spot(k, b, n), :] = run[n]
        if meanwhile is not None:
            meanwhile()
        if k > 0:
            sent(k - 1, b)
        for d in range(1, NX):
            t_copy(k, b, d).wait_recv()
        carry = jnp.zeros((total.shape[0], CH), F32)
        for lag in range(1, NX):
            xs = lax.rem(x + (lag if backward else NX - lag), NX)
            value = tin[k, xs, at, :]
            if lag > 1:
                value = times(value, segs[1 if backward else 0, lag])
            carry = carry + jnp.where(x < NX - lag if backward else x >= lag, value, 0.0)
        for n in range(NZ):
            if n == edge:
                eout[k, spot(k, b, n), :] = carry
            else:
                tile = maps[carry_kind, n + (1 if backward else 0)]
                eout[k, spot(k, b, n), :] = eout[k, spot(k, b, n), :] + times(carry, tile)
        for d in far_first if b == 1 else sooner:
            e_copy(k, b, d).start()
        ein[k, spot(k, b, z), :] = eout[k, spot(k, b, z), :]

    def arrive(k, b):
        for d in far_first[::-1]:
            e_copy(k, b, d).wait_recv()

    def relax(k, b, ahead, old):
        first, last = EDGES[k][b], EDGES[k][b + 1]
        lo = 0 if b == 0 else first + ahead
        hi = SIDE if b == BANDS - 1 else last + ahead
        for p, q in split(lo, hi):
            value = start[px(p, q), :] + STEP * conv(x3a, p, q, ww.at[0])
            mid[px(p, q), :] = value
            fill(x3b, p, q, jnp.tanh(value))
        for p, q in split(first, last):
            value = mid[px(p, q), :] + STEP * conv(x3b, p, q, ww.at[1])
            prop[px(p, q), :] = value
            resout[k, px(p, q), :] = value - old[px(p, q), :]
        send_residual(k, b)


    relax(0, 0, 1, feat)

    def g_pass(d):
        g_copy(d).wait_recv()
        g_forward(d).start()

    each(NZ, g_pass, 1)
    for b in range(1, BANDS):
        relax(0, b, 1, feat)

    each(NZ, lambda d: g_forward(d).wait_recv(), 1)
    made, tiles = {}, {}

    def product(i, j):
        if (i, j) not in made:
            if i == j:
                value = gin[i]
            else:
                step = 1
                while (j // (2 * step)) * 2 * step > i:
                    step *= 2
                m = j // step * step
                value = times(product(i, m - 1), tile_of(m, j))
            made[i, j] = value
        return made[i, j]

    def tile_of(i, j):
        if (i, j) not in tiles:
            value = product(i, j)
            if i == j:
                put(maps, (0, i), value)
                tiles[i, j] = maps.at[0, i]
            elif j == NZ - 1:
                put(maps, (4, i), value)
                tiles[i, j] = maps.at[4, i]
            else:
                n = sum(i2 != j2 and j2 != NZ - 1 for i2, j2 in tiles)
                put(temps, (n,), value)
                tiles[i, j] = temps.at[n]
        return tiles[i, j][...]

    for n in range(NZ):
        tile_of(n, n)
    put(maps, (4, NZ), eye)
    put(maps, (4, NZ - 1), gin[NZ - 1])
    for n in range(NZ - 1):
        tile_of(n, NZ - 1)
    for n in range(NZ):
        prods[1, n] = product(n, NZ - 1)
        prods[0, n + 1] = product(0, n)
        put(maps, (2, n + 1), product(0, n))
    pin[x] = product(0, NZ - 1)

    def p_copy(d):
        return remote(pin.at[x], pin.at[x], p_s.at[d], p_r.at[d], to_x(d))

    each(NX, lambda d: p_copy(d).start(), 1)

    def segments_arrive():
        each(NX, lambda d: p_copy(d).wait_recv(), 1)
        if NX > 2:
            def segment(lag):
                return pin[lax.rem(x + NX + lag, NX)]

            back, ahead = segment(-1), segment(1)
            put(segs, (0, 2), back)
            prods[2, 2] = ahead
            for lag in range(3, NX):
                back = times(segment(1 - lag), segs[0, lag - 1])
                put(segs, (0, lag), back)
                put(segs, (1, lag), segment(lag - 1))
                ahead = times(ahead, segs[1, lag])
                prods[2, lag] = ahead

    def turn_kernels(layer):
        def turn(t):
            block = w[layer, pl.ds(pl.multiple_of((8 - t) * CH, CH), CH), :].astype(F32)
            wt[layer, pl.ds(pl.multiple_of(t * CH, CH), CH), :] = block.T.astype(BF16)
        each(9, turn)
        widen(wwt, layer, wt)

    def first_slot():
        segments_arrive()
        turn_kernels(1)

    for b in range(BANDS):
        scan(0, b, False, (first_slot, lambda: turn_kernels(0), None)[b])

    for b in range(BANDS):
        arrive(0, b)
        for p, q in split(EDGES[0][b], EDGES[0][b + 1]):
            e = ein[0, px(p, q), :]
            ends[px(p, q), :] = prop[px(p, q), :] + times(e, maps[0, z])
            value = start[px(p, q), :] + e
            start[px(p, q), :] = value
            fill(x3a, p, q, jnp.tanh(value))
        relax(1, b, 1, ends)

    def turn_maps(s):
        put(maps, (3, s + 1), prods[0, s + 1].T)

    def second_slot():
        put(maps, (3, 0), eye)
        each(NZ - 1, turn_maps)

    def third_slot():
        loads[3].wait()
        for p, q in split(0, SIDE):
            fill(z3a, p, q, cot[px(p, q), :])
        for p, q in split(0, SIDE):
            ycot[px(p, q), :] = conv(z3a, p, q, wwt.at[1])

    for b in range(BANDS):
        scan(1, b, False, (second_slot, third_slot, None)[b])

    def pull(k, b, old):
        first, last = EDGES[k][b], EDGES[k][b + 1]
        for p, q in split(first, last):
            value = mid[px(p, q), :] + d0[px(p, q), :] * conv(z3b, p, q, wwt.at[0])
            prop[px(p, q), :] = value
            resout[k, px(p, q), :] = value - old[px(p, q), :]
        send_residual(k, b)

    def behind(k, b):
        lo = 0 if b == 0 else EDGES[k][b] + 1
        hi = SIDE if b == BANDS - 1 else EDGES[k][b + 1] + 1
        return split(lo, hi)

    for b in range(BANDS):
        arrive(1, b)
        for p, q in split(EDGES[1][b], EDGES[1][b + 1]):
            e = ein[1, px(p, q), :]
            ends[px(p, q), :] = prop[px(p, q), :] + times(e, maps[0, z])
            value = start[px(p, q), :] + e
            start[px(p, q), :] = value
            active = jnp.tanh(value)
            d0[px(p, q), :] = STEP * (1.0 - active * active)
            fill(x3a, p, q, active)
        for p, q in behind(2, b):
            active = jnp.tanh(start[px(p, q), :] + STEP * conv(x3a, p, q, ww.at[0]))
            slope = STEP * (1.0 - active * active)
            d1[px(p, q), :] = slope
            fill(x3b, p, q, active)
            value = cot[px(p, q), :] + slope * ycot[px(p, q), :]
            mid[px(p, q), :] = value
            fill(z3b, p, q, value)
        pull(2, b, cot)

    def turn_steps(s):
        put(maps, (1, s), gin[s].T)

    def turn_carries(s):
        put(maps, (5, s), prods[1, s].T)

    def fourth_slot():
        each(NZ, turn_carries)
        each(NZ, lambda d: g_copy(d).wait_send(), 1)
        each(NZ, lambda d: g_forward(d).wait_send(), 1)
        each(NX, lambda d: p_copy(d).wait_send(), 1)
        for lag in range(2, NX):
            put(segs, (1, lag), prods[2, lag].T)

    each(NZ, turn_steps)
    for b in range(BANDS):
        scan(2, b, True, (fourth_slot, None, None)[b])

    for b in range(BANDS):
        arrive(2, b)
        for p, q in split(EDGES[2][b], EDGES[2][b + 1]):
            f = ein[2, px(p, q), :]
            adj[px(p, q), :] = prop[px(p, q), :] + times(f, maps[1, z])
            value = cot[px(p, q), :] + f
            start[px(p, q), :] = value
            fill(z3a, p, q, value)
        for p, q in behind(3, b):
            value = start[px(p, q), :] + d1[px(p, q), :] * conv(z3a, p, q, wwt.at[1])
            mid[px(p, q), :] = value
            fill(z3b, p, q, value)
        pull(3, b, adj)

    for b in range(BANDS):
        scan(3, b, True)

    def place(core, yy):
        return pl.ds(pl.multiple_of(core * half + yy * part, part), part)

    other = pl.ds(pl.multiple_of((NC - 1 - c) * half, half), half)

    def sib_copy(layer):
        return remote(local_grad.at[layer, other], gs.at[layer], sib_s.at[layer], sib_r.at[layer], to_core())

    def rs_copy(layer, d):
        return remote(hsum.at[layer, lax.rem(y + d, NY)], yin.at[layer, d], rs_s.at[layer, d], rs_r.at[layer, d], to_y(d))

    def ag_copy(layer, d):
        at = place(c, y)
        return remote(grad.at[layer, at], grad.at[layer, at], ag_s.at[layer, d], ag_r.at[layer, d], to_y(d))

    def fw_copy(layer, d):
        at = place(c, lax.rem(y + NY - d, NY))
        return remote(grad.at[layer, at], grad.at[layer, at], fw_s.at[layer, d], fw_r.at[layer, d], to_core())

    def reduce_core(layer):
        sib_copy(layer).wait()
        for yy in range(NY):
            hsum[layer, yy] = local_grad[layer, place(c, yy), :] + gs[layer, pl.ds(yy * part, part), :]
        each(NY, lambda d: rs_copy(layer, d).start(), 1)

    def reduce_chips(layer):
        total = hsum[layer, y]
        for d in range(1, NY):
            rs_copy(layer, d).wait_recv()
            total = total + yin[layer, d]
        grad[layer, place(c, y), :] = total * factor
        each(NY, lambda d: ag_copy(layer, d).start(), 1)
        fw_copy(layer, 0).start()

    def spread(layer):
        def go(d):
            ag_copy(layer, d).wait_recv()
            fw_copy(layer, d).start()
        each(NY, go, 1)

    def gradient(layer, signal, buffer, first, last, more):
        for r in range(3):
            block = jnp.dot(signal[:, px(first, last)], buffer[px(first + r, last + r), :], preferred_element_type=F32)
            for s in range(3):
                t = 3 * r + s
                value = block[:, CH * s : CH * (s + 1)].T
                at = slice(CH * t, CH * (t + 1))
                local_grad[layer, at, :] = local_grad[layer, at, :] + value if more else value

    def adjoint_out(b):
        for p, q in split(EDGES[3][b], EDGES[3][b + 1]):
            adj[px(p, q), :] = prop[px(p, q), :] + times(ein[3, px(p, q), :], maps[1, z])

    def top_signal(p, q):
        value = start[px(p, q), :] + ein[3, px(p, q), :]
        start[px(p, q), :] = value
        fill(z3a, p, q, value)
        zt[:, px(p, q)] = value.T.astype(BF16)

    def lower_signal(p, q):
        value = start[px(p, q), :] + d1[px(p, q), :] * conv(z3a, p, q, wwt.at[1])
        zt0[:, px(p, q)] = value.T.astype(BF16)

    cuts = [e // 4 * 4 for e in EDGES[3]]
    lows = [0] + [(e - 1) // 4 * 4 for e in cuts[1:-1]] + [SIDE]

    def halves(first, last):
        middle = (first + last) // 8 * 4
        return [(p, q) for p, q in ((first, middle), (middle, last)) if q > p]

    for b in range(BANDS):
        arrive(3, b)
        for p, q in halves(cuts[b], cuts[b + 1]):
            top_signal(p, q)
        gradient(1, zt, x3b, cuts[b], cuts[b + 1], b > 0)
        if b == BANDS - 1:
            sib_copy(1).start()
        for p, q in halves(lows[b], lows[b + 1]):
            lower_signal(p, q)
        if b == BANDS - 1:
            reduce_core(1)
        gradient(0, zt0, x3a, lows[b], lows[b + 1], b > 0)
        if b < BANDS - 1:
            adjoint_out(b)
    sib_copy(0).start()
    adjoint_out(BANDS - 1)
    reduce_core(0)
    reduce_chips(1)
    reduce_chips(0)
    for b in range(BANDS):
        sent(3, b)
    spread(1)
    spread(0)
    for layer in range(2):
        each(NY, lambda d: fw_copy(layer, d).wait_recv(), 0)

    for layer in range(2):
        each(NY, lambda d: rs_copy(layer, d).wait_send(), 1)
        each(NY, lambda d: ag_copy(layer, d).wait_send(), 1)
        each(NY, lambda d: fw_copy(layer, d).wait_send(), 0)


def make_local(NX, NZ, NY, NC):
    half = TAPS // NC
    part = half // NY
    dma = pltpu.SemaphoreType.DMA
    vmem = pltpu.VMEM
    image = vmem((PIXELS, CH), F32)
    padded = vmem((PIXELS + 2 * SIDE, 3 * CH), BF16)
    sweeps = vmem((4, PIXELS, CH), F32)
    moves = dma((4 * BANDS, NZ))

    def local(features, cotangent, weights, coarse_map):
        factor = STEP / (features.shape[0] * NY * NC)
        out = pl.pallas_call(
            functools.partial(body, NX, NZ, NY, NC, factor),
            out_shape=(
                jax.ShapeDtypeStruct((PIXELS, CH), F32),
                jax.ShapeDtypeStruct((PIXELS, CH), F32),
                jax.ShapeDtypeStruct((2, TAPS, CH), F32),
            ),
            in_specs=[pl.BlockSpec(memory_space=pltpu.HBM)] * 4,
            out_specs=[pl.BlockSpec(memory_space=vmem)] * 3,
            scratch_shapes=[
                image, image, vmem((2, TAPS, CH), BF16), vmem((CH, CH), F32),
                padded, padded, padded, padded,
                vmem((2, TAPS, CH), BF16),
                vmem((2, 12 * CH, 2 * CH), BF16), vmem((2, 12 * CH, 2 * CH), BF16),
                image, image, image, image, image, image,
                vmem((CH, PIXELS), BF16), vmem((CH, PIXELS), BF16),
                sweeps, sweeps, sweeps, sweeps,
                vmem((4, NX, PIXELS // NZ, CH), F32),
                vmem((NZ, CH, CH), F32),
                vmem((NX, CH, CH), F32),
                vmem((3, max(NX, NZ + 1), CH, CH), F32),
                vmem((NZ, 2 * CH, 2 * CH), BF16),
                vmem((6, NZ + 1, 2 * CH, 2 * CH), BF16),
                vmem((2, NX, 2 * CH, 2 * CH), BF16),
                vmem((2, TAPS, CH), F32),
                vmem((2, half, CH), F32),
                vmem((2, NY, part, CH), F32),
                vmem((2, NY, part, CH), F32),
                dma((4,)),
                moves, moves, moves, moves, dma((4 * BANDS, NX)), dma((4 * BANDS, NX)),
                dma((NZ,)), dma((NZ,)), dma((NZ,)), dma((NZ,)), dma((NX,)), dma((NX,)),
                dma((2,)), dma((2,)), dma((2, NY)), dma((2, NY)), dma((2, NY)), dma((2, NY)), dma((2, NY)), dma((2, NY)),
            ],
            compiler_params=pltpu.CompilerParams(
                collective_id=0, has_side_effects=True, vmem_limit_bytes=56 * 1024 * 1024
            ),
            cost_estimate=pl.CostEstimate(flops=5 * 10**9, bytes_accessed=5 * 10**6, transcendentals=10**6),
        )(
            features.reshape(PIXELS, CH),
            cotangent.reshape(PIXELS, CH),
            weights.reshape(2, TAPS, CH),
            coarse_map.reshape(CH, CH),
        )
        shape = (1, 1, SIDE, SIDE, CH)
        return out[0].reshape(shape), out[1].reshape(shape), out[2].reshape(2, 9, CH, CH)

    return local


def build(mesh, sizes):
    return jax.shard_map(
        make_local(*sizes),
        mesh=mesh,
        in_specs=(P("dp", None, None, None), P("dp", None, None, None), P("tm", None, None, None), P("tm", None, None)),
        out_specs=(P("tm", "dp", None, None, None), P("tm", "dp", None, None, None), P("tm", None, None, None)),
        check_vma=False,
    )


def solution(mesh):
    return build(mesh, (4, 8, 4, 2))
```

```python
import functools

import jax
import jax.numpy as jnp
from jax import lax
from jax.experimental import pallas as pl
from jax.experimental.pallas import tpu as pltpu
from jax.sharding import PartitionSpec as P

MESH = pl.DeviceIdType.MESH
STEP = 0.25
DIAGONAL = 0.9
SIDE = 32
PIXELS = SIDE * SIDE
CH = 128
BANDS = 2
EDGES = ((0, 20, 32), (0, 18, 32), (0, 16, 32), (0, 14, 32))
TAPS = 9 * CH
F32, BF16 = jnp.float32, jnp.bfloat16


def two_terms(value):
    high = value.astype(BF16)
    return high, (value - high.astype(F32)).astype(BF16)


def times(value, tile):
    high, low = two_terms(value)
    both = jnp.dot(jnp.concatenate([high, low], 1), tile, preferred_element_type=F32)
    return both[:, :CH] + both[:, CH:]


def split(first, last, most=12):
    count = -(-(last - first) // most)
    cuts = [first + (last - first) * n // (2 * count) * 2 for n in range(count)] + [last]
    return list(zip(cuts[:-1], cuts[1:]))


def body(
    NX, NZ, NY, NC, factor,
    feat_in, cot_in, w_in, cm_in,
    ends, adj, grad,
    feat, cot, w, cm,
    x3a, x3b, z3a, z3b, wt, ww, wwt, start, mid, prop, d0, d1, ycot, zt, zt0,
    resout, resin, eout, ein, tin, gin, pin, prods, temps, maps, segs, local_grad, gs, hsum, yin,
    in_s,
    res_s, res_r, e_s, e_r, t_s, t_r, g_s, g_r, gf_s, gf_r, p_s, p_r, sib_s, sib_r, rs_s, rs_r, ag_s, ag_r, fw_s, fw_r,
):
    loads = [
        pltpu.make_async_copy(src, dst, in_s.at[n])
        for n, (src, dst) in enumerate(((cm_in, cm), (feat_in, feat), (w_in, w), (cot_in, cot)))
    ]
    for load in loads:
        load.start()

    tm, dp = lax.axis_index("tm"), lax.axis_index("dp")
    x, z = tm // NZ, lax.rem(tm, NZ)
    y, c = dp // NC, lax.rem(dp, NC)
    half = TAPS // NC
    part = half // NY
    near_first = sorted(range(1, NZ), key=lambda d: min(d, NZ - d))

    def to_z(d):
        return {"tm": x * NZ + lax.rem(z + d, NZ)}

    def to_x(d):
        return {"tm": lax.rem(x + d, NX) * NZ + z}

    def to_y(d):
        return {"dp": lax.rem(y + d, NY) * NC + c}

    def to_core():
        return {"dp": y * NC + (NC - 1 - c)}

    def remote(src, dst, send, recv, device):
        return pltpu.make_async_remote_copy(
            src_ref=src, dst_ref=dst, send_sem=send, recv_sem=recv, device_id=device, device_id_type=MESH
        )

    def each(count, f, first=0):
        def go(i, carry):
            f(i)
            return carry
        lax.fori_loop(first, count, go, 0)

    barrier = pltpu.get_barrier_semaphore()

    def greet(device):
        pl.semaphore_signal(barrier, inc=1, device_id=device, device_id_type=MESH)

    each(NZ, lambda d: greet(to_z(d)), 1)
    each(NX, lambda d: greet(to_x(d)), 1)
    each(NY, lambda d: greet(to_y(d)), 1)
    greet(to_core())

    def px(first, last):
        return slice(first * SIDE, last * SIDE)

    def fill(buffer, first, last, value):
        size = (last - first) * SIDE
        column = lax.rem(lax.broadcasted_iota(jnp.int32, (size, CH), 0), SIDE)
        left = jnp.where(column == 0, 0.0, pltpu.roll(value, 1, 0))
        right = jnp.where(column == SIDE - 1, 0.0, pltpu.roll(value, size - 1, 0))
        at = px(first + 1, last + 1)
        buffer[at, :CH] = left.astype(BF16)
        buffer[at, CH : 2 * CH] = value.astype(BF16)
        buffer[at, 2 * CH :] = right.astype(BF16)

    def conv(buffer, first, last, kernel):
        odd = (last - first) % 2
        top = first - odd if last == SIDE else first
        pairs = range((last - first + odd) // 2)
        pieces = [
            jnp.concatenate([buffer[px(top + 2 * m + r, top + 2 * m + r + 1), :] for m in pairs], 0) for r in range(4)
        ]
        both = jnp.dot(jnp.concatenate(pieces, 1), kernel[...], preferred_element_type=F32)
        rows = [both[px(m, m + 1), CH * h : CH * (h + 1)] for m in pairs for h in range(2)]
        return jnp.concatenate(rows[first - top : last - top], 0)

    def widen(wide, layer, source):
        for r in range(4):
            at = slice(3 * CH * r, 3 * CH * (r + 1))
            zero = jnp.zeros((3 * CH, CH), BF16)
            wide[layer, at, :CH] = source[layer, 3 * CH * r : 3 * CH * (r + 1), :] if r < 3 else zero
            wide[layer, at, CH:] = source[layer, 3 * CH * (r - 1) : 3 * CH * r, :] if r > 0 else zero

    zero_row = jnp.zeros((SIDE, 3 * CH), BF16)
    for buffer in (x3a, x3b, z3a, z3b):
        buffer[:SIDE, :] = zero_row
        buffer[PIXELS + SIDE :, :] = zero_row
    eye = (lax.broadcasted_iota(jnp.int32, (CH, CH), 0) == lax.broadcasted_iota(jnp.int32, (CH, CH), 1)).astype(F32)
    loads[0].wait()
    gin[z] = DIAGONAL * eye + cm[...]

    loads[1].wait()
    for p, q in split(0, SIDE):
        value = feat[px(p, q), :]
        start[px(p, q), :] = value
        fill(x3a, p, q, jnp.tanh(value))
    loads[2].wait()
    widen(ww, 0, w)
    widen(ww, 1, w)
    pl.semaphore_wait(barrier, NZ - 1 + NX - 1 + NY - 1 + 1)

    gh = pl.ds(pl.multiple_of(c * (CH // NC), CH // NC), CH // NC)

    def g_copy(d):
        return remote(gin.at[z, gh], gin.at[z, gh], g_s.at[d], g_r.at[d], to_z(d))

    def g_forward(d):
        zs = lax.rem(z + NZ - d, NZ)
        return remote(gin.at[zs, gh], gin.at[zs, gh], gf_s.at[d], gf_r.at[d], to_core())

    for d in near_first:
        g_copy(d).start()

    def share(k, b):
        first, last = EDGES[k][b], EDGES[k][b + 1]
        return first * SIDE, (last - first) * SIDE // NZ

    def spot(k, b, n):
        base, R = share(k, b)
        if isinstance(n, int):
            return slice(base + n * R, base + n * R + R)
        return pl.ds(pl.multiple_of(base + n * R, 8), R)

    def res_copy(k, b, d):
        zp = lax.rem(z + d, NZ)
        m = BANDS * k + b
        return remote(
            resout.at[k, spot(k, b, zp)], resin.at[k, spot(k, b, z)], res_s.at[m, d], res_r.at[m, d], to_z(d)
        )

    def send_residual(k, b):
        for d in near_first:
            res_copy(k, b, d).start()
        resin[k, spot(k, b, z), :] = resout[k, spot(k, b, z), :]

    def t_spot(k, b):
        base, R = share(k, b)
        return slice(base // NZ, base // NZ + R)

    def t_copy(k, b, d):
        m = BANDS * k + b
        at = t_spot(k, b)
        return remote(tin.at[k, x, at], tin.at[k, x, at], t_s.at[m, d], t_r.at[m, d], to_x(d))

    def e_copy(k, b, d):
        zp = lax.rem(z + d, NZ)
        m = BANDS * k + b
        return remote(eout.at[k, spot(k, b, zp)], ein.at[k, spot(k, b, z)], e_s.at[m, d], e_r.at[m, d], to_z(d))

    def put(where, index, matrix):
        high, low = two_terms(matrix)
        where[(*index, slice(0, CH), slice(0, CH))] = high
        where[(*index, slice(0, CH), slice(CH, None))] = low
        where[(*index, slice(CH, None), slice(0, CH))] = high
        where[(*index, slice(CH, None), slice(CH, None))] = jnp.zeros((CH, CH), BF16)

    def sent(k, b):
        for d in near_first:
            res_copy(k, b, d).wait_send()
            e_copy(k, b, d).wait_send()
        for d in range(1, NX):
            t_copy(k, b, d).wait_send()

    def scan(k, b, backward, meanwhile=None):
        total_kind, chain_kind, carry_kind = (3, 1, 5) if backward else (4, 0, 2)
        at = t_spot(k, b)
        edge = NZ - 1 if backward else 0

        def term(d):
            s = lax.rem(z + NZ - d, NZ)
            return times(resin[k, spot(k, b, s), :], maps[total_kind, s + (0 if backward else 1)])

        near = near_first[: NZ // 2]
        for d in near:
            res_copy(k, b, d).wait_recv()
        total = term(0)
        for d in near:
            total = total + term(d)
        for d in near_first[NZ // 2 :]:
            res_copy(k, b, d).wait_recv()
        for d in near_first[NZ // 2 :]:
            total = total + term(d)
        tin[k, x, at, :] = total
        for d in range(1, NX):
            t_copy(k, b, d).start()
        run = {}
        if backward:
            value = resin[k, spot(k, b, NZ - 1), :]
            run[NZ - 2] = value
            for s in range(NZ - 2, 0, -1):
                value = times(value, maps[chain_kind, s]) + resin[k, spot(k, b, s), :]
                run[s - 1] = value
        else:
            value = resin[k, spot(k, b, 0), :]
            run[1] = value
            for s in range(1, NZ - 1):
                value = times(value, maps[chain_kind, s]) + resin[k, spot(k, b, s), :]
                run[s + 1] = value
        for n in run:
            eout[k, spot(k, b, n), :] = run[n]
        if meanwhile is not None:
            meanwhile()
        if k > 0:
            sent(k - 1, b)
        for d in range(1, NX):
            t_copy(k, b, d).wait_recv()
        carry = jnp.zeros((total.shape[0], CH), F32)
        for lag in range(1, NX):
            xs = lax.rem(x + (lag if backward else NX - lag), NX)
            value = tin[k, xs, at, :]
            if lag > 1:
                value = times(value, segs[1 if backward else 0, lag])
            carry = carry + jnp.where(x < NX - lag if backward else x >= lag, value, 0.0)
        for n in range(NZ):
            if n == edge:
                eout[k, spot(k, b, n), :] = carry
            else:
                tile = maps[carry_kind, n + (1 if backward else 0)]
                eout[k, spot(k, b, n), :] = eout[k, spot(k, b, n), :] + times(carry, tile)
        for d in near_first:
            e_copy(k, b, d).start()
        ein[k, spot(k, b, z), :] = eout[k, spot(k, b, z), :]

    def arrive(k, b):
        for d in near_first:
            e_copy(k, b, d).wait_recv()

    def relax(k, b, ahead, old):
        first, last = EDGES[k][b], EDGES[k][b + 1]
        lo = 0 if b == 0 else first + ahead
        hi = SIDE if b == BANDS - 1 else last + ahead
        for p, q in split(lo, hi):
            value = start[px(p, q), :] + STEP * conv(x3a, p, q, ww.at[0])
            mid[px(p, q), :] = value
            fill(x3b, p, q, jnp.tanh(value))
        for p, q in split(first, last):
            value = mid[px(p, q), :] + STEP * conv(x3b, p, q, ww.at[1])
            prop[px(p, q), :] = value
            resout[k, px(p, q), :] = value - old[px(p, q), :]
        send_residual(k, b)


    relax(0, 0, 1, feat)

    def g_pass(d):
        g_copy(d).wait_recv()
        g_forward(d).start()

    each(NZ, g_pass, 1)
    for b in range(1, BANDS):
        relax(0, b, 1, feat)

    each(NZ, lambda d: g_forward(d).wait_recv(), 1)
    made, tiles = {}, {}

    def product(i, j):
        if (i, j) not in made:
            if i == j:
                value = gin[i]
            else:
                step = 1
                while (j // (2 * step)) * 2 * step > i:
                    step *= 2
                m = j // step * step
                value = times(product(i, m - 1), tile_of(m, j))
            made[i, j] = value
        return made[i, j]

    def tile_of(i, j):
        if (i, j) not in tiles:
            value = product(i, j)
            if i == j:
                put(maps, (0, i), value)
                tiles[i, j] = maps.at[0, i]
            elif j == NZ - 1:
                put(maps, (4, i), value)
                tiles[i, j] = maps.at[4, i]
            else:
                n = sum(i2 != j2 and j2 != NZ - 1 for i2, j2 in tiles)
                put(temps, (n,), value)
                tiles[i, j] = temps.at[n]
        return tiles[i, j][...]

    for n in range(NZ):
        tile_of(n, n)
    put(maps, (4, NZ), eye)
    put(maps, (4, NZ - 1), gin[NZ - 1])
    for n in range(NZ - 1):
        tile_of(n, NZ - 1)
    for n in range(NZ):
        prods[1, n] = product(n, NZ - 1)
        prods[0, n + 1] = product(0, n)
        put(maps, (2, n + 1), product(0, n))
    pin[x] = product(0, NZ - 1)

    def p_copy(d):
        return remote(pin.at[x], pin.at[x], p_s.at[d], p_r.at[d], to_x(d))

    each(NX, lambda d: p_copy(d).start(), 1)

    def segments_arrive():
        each(NX, lambda d: p_copy(d).wait_recv(), 1)
        if NX > 2:
            def segment(lag):
                return pin[lax.rem(x + NX + lag, NX)]

            back, ahead = segment(-1), segment(1)
            put(segs, (0, 2), back)
            prods[2, 2] = ahead
            for lag in range(3, NX):
                back = times(segment(1 - lag), segs[0, lag - 1])
                put(segs, (0, lag), back)
                put(segs, (1, lag), segment(lag - 1))
                ahead = times(ahead, segs[1, lag])
                prods[2, lag] = ahead

    def turn_kernels(layer):
        def turn(t):
            block = w[layer, pl.ds(pl.multiple_of((8 - t) * CH, CH), CH), :].astype(F32)
            wt[layer, pl.ds(pl.multiple_of(t * CH, CH), CH), :] = block.T.astype(BF16)
        each(9, turn)
        widen(wwt, layer, wt)

    def first_slot():
        segments_arrive()
        turn_kernels(1)

    for b in range(BANDS):
        scan(0, b, False, (first_slot, lambda: turn_kernels(0), None)[b])

    for b in range(BANDS):
        arrive(0, b)
        for p, q in split(EDGES[0][b], EDGES[0][b + 1]):
            e = ein[0, px(p, q), :]
            ends[px(p, q), :] = prop[px(p, q), :] + times(e, maps[0, z])
            value = start[px(p, q), :] + e
            start[px(p, q), :] = value
            fill(x3a, p, q, jnp.tanh(value))
        relax(1, b, 1, ends)

    def turn_maps(s):
        put(maps, (3, s + 1), prods[0, s + 1].T)

    def second_slot():
        put(maps, (3, 0), eye)
        each(NZ - 1, turn_maps)

    def third_slot():
        loads[3].wait()
        for p, q in split(0, SIDE):
            fill(z3a, p, q, cot[px(p, q), :])
        for p, q in split(0, SIDE):
            ycot[px(p, q), :] = conv(z3a, p, q, wwt.at[1])

    for b in range(BANDS):
        scan(1, b, False, (second_slot, third_slot, None)[b])

    def pull(k, b, old):
        first, last = EDGES[k][b], EDGES[k][b + 1]
        for p, q in split(first, last):
            value = mid[px(p, q), :] + d0[px(p, q), :] * conv(z3b, p, q, wwt.at[0])
            prop[px(p, q), :] = value
            resout[k, px(p, q), :] = value - old[px(p, q), :]
        send_residual(k, b)

    def behind(k, b):
        lo = 0 if b == 0 else EDGES[k][b] + 1
        hi = SIDE if b == BANDS - 1 else EDGES[k][b + 1] + 1
        return split(lo, hi)

    for b in range(BANDS):
        arrive(1, b)
        for p, q in split(EDGES[1][b], EDGES[1][b + 1]):
            e = ein[1, px(p, q), :]
            ends[px(p, q), :] = prop[px(p, q), :] + times(e, maps[0, z])
            value = start[px(p, q), :] + e
            start[px(p, q), :] = value
            active = jnp.tanh(value)
            d0[px(p, q), :] = STEP * (1.0 - active * active)
            fill(x3a, p, q, active)
        for p, q in behind(2, b):
            active = jnp.tanh(start[px(p, q), :] + STEP * conv(x3a, p, q, ww.at[0]))
            slope = STEP * (1.0 - active * active)
            d1[px(p, q), :] = slope
            fill(x3b, p, q, active)
            value = cot[px(p, q), :] + slope * ycot[px(p, q), :]
            mid[px(p, q), :] = value
            fill(z3b, p, q, value)
        pull(2, b, cot)

    def turn_steps(s):
        put(maps, (1, s), gin[s].T)

    def turn_carries(s):
        put(maps, (5, s), prods[1, s].T)

    def fourth_slot():
        each(NZ, turn_carries)
        each(NZ, lambda d: g_copy(d).wait_send(), 1)
        each(NZ, lambda d: g_forward(d).wait_send(), 1)
        each(NX, lambda d: p_copy(d).wait_send(), 1)
        for lag in range(2, NX):
            put(segs, (1, lag), prods[2, lag].T)

    each(NZ, turn_steps)
    for b in range(BANDS):
        scan(2, b, True, (fourth_slot, None, None)[b])

    for b in range(BANDS):
        arrive(2, b)
        for p, q in split(EDGES[2][b], EDGES[2][b + 1]):
            f = ein[2, px(p, q), :]
            adj[px(p, q), :] = prop[px(p, q), :] + times(f, maps[1, z])
            value = cot[px(p, q), :] + f
            start[px(p, q), :] = value
            fill(z3a, p, q, value)
        for p, q in behind(3, b):
            value = start[px(p, q), :] + d1[px(p, q), :] * conv(z3a, p, q, wwt.at[1])
            mid[px(p, q), :] = value
            fill(z3b, p, q, value)
        pull(3, b, adj)

    for b in range(BANDS):
        scan(3, b, True)

    def place(core, yy):
        return pl.ds(pl.multiple_of(core * half + yy * part, part), part)

    other = pl.ds(pl.multiple_of((NC - 1 - c) * half, half), half)

    def sib_copy(layer):
        return remote(local_grad.at[layer, other], gs.at[layer], sib_s.at[layer], sib_r.at[layer], to_core())

    def rs_copy(layer, d):
        return remote(hsum.at[layer, lax.rem(y + d, NY)], yin.at[layer, d], rs_s.at[layer, d], rs_r.at[layer, d], to_y(d))

    def ag_copy(layer, d):
        at = place(c, y)
        return remote(grad.at[layer, at], grad.at[layer, at], ag_s.at[layer, d], ag_r.at[layer, d], to_y(d))

    def fw_copy(layer, d):
        at = place(c, lax.rem(y + NY - d, NY))
        return remote(grad.at[layer, at], grad.at[layer, at], fw_s.at[layer, d], fw_r.at[layer, d], to_core())

    def reduce_core(layer):
        sib_copy(layer).wait()
        for yy in range(NY):
            hsum[layer, yy] = local_grad[layer, place(c, yy), :] + gs[layer, pl.ds(yy * part, part), :]
        each(NY, lambda d: rs_copy(layer, d).start(), 1)

    def reduce_chips(layer):
        total = hsum[layer, y]
        for d in range(1, NY):
            rs_copy(layer, d).wait_recv()
            total = total + yin[layer, d]
        grad[layer, place(c, y), :] = total * factor
        each(NY, lambda d: ag_copy(layer, d).start(), 1)
        fw_copy(layer, 0).start()

    def spread(layer):
        def go(d):
            ag_copy(layer, d).wait_recv()
            fw_copy(layer, d).start()
        each(NY, go, 1)

    def gradient(layer, signal, buffer, first, last, more):
        for r in range(3):
            block = jnp.dot(signal[:, px(first, last)], buffer[px(first + r, last + r), :], preferred_element_type=F32)
            for s in range(3):
                t = 3 * r + s
                value = block[:, CH * s : CH * (s + 1)].T
                at = slice(CH * t, CH * (t + 1))
                local_grad[layer, at, :] = local_grad[layer, at, :] + value if more else value

    def adjoint_out(b):
        for p, q in split(EDGES[3][b], EDGES[3][b + 1]):
            adj[px(p, q), :] = prop[px(p, q), :] + times(ein[3, px(p, q), :], maps[1, z])

    def top_signal(p, q):
        value = start[px(p, q), :] + ein[3, px(p, q), :]
        start[px(p, q), :] = value
        fill(z3a, p, q, value)
        zt[:, px(p, q)] = value.T.astype(BF16)

    def lower_signal(p, q):
        value = start[px(p, q), :] + d1[px(p, q), :] * conv(z3a, p, q, wwt.at[1])
        zt0[:, px(p, q)] = value.T.astype(BF16)

    cuts = [e // 4 * 4 for e in EDGES[3]]
    lows = [0] + [(e - 1) // 4 * 4 for e in cuts[1:-1]] + [SIDE]

    def halves(first, last):
        middle = (first + last) // 8 * 4
        return [(p, q) for p, q in ((first, middle), (middle, last)) if q > p]

    for b in range(BANDS):
        arrive(3, b)
        for p, q in halves(cuts[b], cuts[b + 1]):
            top_signal(p, q)
        gradient(1, zt, x3b, cuts[b], cuts[b + 1], b > 0)
        if b == BANDS - 1:
            sib_copy(1).start()
        for p, q in halves(lows[b], lows[b + 1]):
            lower_signal(p, q)
        if b == BANDS - 1:
            reduce_core(1)
        gradient(0, zt0, x3a, lows[b], lows[b + 1], b > 0)
        if b < BANDS - 1:
            adjoint_out(b)
    sib_copy(0).start()
    adjoint_out(BANDS - 1)
    reduce_core(0)
    reduce_chips(1)
    reduce_chips(0)
    for b in range(BANDS):
        sent(3, b)
    spread(1)
    spread(0)
    for layer in range(2):
        each(NY, lambda d: fw_copy(layer, d).wait_recv(), 0)

    for layer in range(2):
        each(NY, lambda d: rs_copy(layer, d).wait_send(), 1)
        each(NY, lambda d: ag_copy(layer, d).wait_send(), 1)
        each(NY, lambda d: fw_copy(layer, d).wait_send(), 0)


def make_local(NX, NZ, NY, NC):
    half = TAPS // NC
    part = half // NY
    dma = pltpu.SemaphoreType.DMA
    vmem = pltpu.VMEM
    image = vmem((PIXELS, CH), F32)
    padded = vmem((PIXELS + 2 * SIDE, 3 * CH), BF16)
    sweeps = vmem((4, PIXELS, CH), F32)
    moves = dma((4 * BANDS, NZ))

    def local(features, cotangent, weights, coarse_map):
        factor = STEP / (features.shape[0] * NY * NC)
        out = pl.pallas_call(
            functools.partial(body, NX, NZ, NY, NC, factor),
            out_shape=(
                jax.ShapeDtypeStruct((PIXELS, CH), F32),
                jax.ShapeDtypeStruct((PIXELS, CH), F32),
                jax.ShapeDtypeStruct((2, TAPS, CH), F32),
            ),
            in_specs=[pl.BlockSpec(memory_space=pltpu.HBM)] * 4,
            out_specs=[pl.BlockSpec(memory_space=vmem)] * 3,
            scratch_shapes=[
                image, image, vmem((2, TAPS, CH), BF16), vmem((CH, CH), F32),
                padded, padded, padded, padded,
                vmem((2, TAPS, CH), BF16),
                vmem((2, 12 * CH, 2 * CH), BF16), vmem((2, 12 * CH, 2 * CH), BF16),
                image, image, image, image, image, image,
                vmem((CH, PIXELS), BF16), vmem((CH, PIXELS), BF16),
                sweeps, sweeps, sweeps, sweeps,
                vmem((4, NX, PIXELS // NZ, CH), F32),
                vmem((NZ, CH, CH), F32),
                vmem((NX, CH, CH), F32),
                vmem((3, max(NX, NZ + 1), CH, CH), F32),
                vmem((NZ, 2 * CH, 2 * CH), BF16),
                vmem((6, NZ + 1, 2 * CH, 2 * CH), BF16),
                vmem((2, NX, 2 * CH, 2 * CH), BF16),
                vmem((2, TAPS, CH), F32),
                vmem((2, half, CH), F32),
                vmem((2, NY, part, CH), F32),
                vmem((2, NY, part, CH), F32),
                dma((4,)),
                moves, moves, moves, moves, dma((4 * BANDS, NX)), dma((4 * BANDS, NX)),
                dma((NZ,)), dma((NZ,)), dma((NZ,)), dma((NZ,)), dma((NX,)), dma((NX,)),
                dma((2,)), dma((2,)), dma((2, NY)), dma((2, NY)), dma((2, NY)), dma((2, NY)), dma((2, NY)), dma((2, NY)),
            ],
            compiler_params=pltpu.CompilerParams(
                collective_id=0, has_side_effects=True, vmem_limit_bytes=56 * 1024 * 1024
            ),
            cost_estimate=pl.CostEstimate(flops=5 * 10**9, bytes_accessed=5 * 10**6, transcendentals=10**6),
        )(
            features.reshape(PIXELS, CH),
            cotangent.reshape(PIXELS, CH),
            weights.reshape(2, TAPS, CH),
            coarse_map.reshape(CH, CH),
        )
        shape = (1, 1, SIDE, SIDE, CH)
        return out[0].reshape(shape), out[1].reshape(shape), out[2].reshape(2, 9, CH, CH)

    return local


def build(mesh, sizes):
    return jax.shard_map(
        make_local(*sizes),
        mesh=mesh,
        in_specs=(P("dp", None, None, None), P("dp", None, None, None), P("tm", None, None, None), P("tm", None, None)),
        out_specs=(P("tm", "dp", None, None, None), P("tm", "dp", None, None, None), P("tm", None, None, None)),
        check_vma=False,
    )


def solution(mesh):
    return build(mesh, (4, 8, 4, 2))
```
